256 devices in a mesh: sec: 16 (over z, core), tile: 16 (over y, x).
Axes of the slice: x: 4, y: 4, z: 8, core: 2. Of those that a mesh axis runs over, the one named last changes fastest.
Arguments:
- raw_sections: bfloat16 [32, 128, 2048], P('sec', None, 'tile'), may hold values from -6 to 6
- shift_cols: int32 [32], P('sec'), may hold values from -64 to 63
- shift_rows: int32 [32], P('sec'), may hold values from -2 to 1
- w_first: bfloat16 [32, 1, 3, 3], replicated, may hold values from -2 to 2
- b_first: float32 [32], replicated, may hold values from -3 to 3
- w_second: bfloat16 [32, 32, 3, 3], replicated, may hold values from -0.375 to 0.375
- b_second: float32 [32], replicated, may hold values from -3 to 3
- w_stride: bfloat16 [32, 32, 2, 2], replicated, may hold values from -0.5 to 0.5
- b_stride: float32 [32], replicated, may hold values from -3 to 3
- w_depth: bfloat16 [64, 32, 3, 3, 3], replicated, may hold values from -0.21875 to 0.21875
- b_depth: float32 [64], replicated, may hold values from -3 to 3
- w_head: float32 [3, 64], replicated, may hold values from -0.75 to 0.75
- b_head: float32 [3], replicated, may hold values from -3 to 3
Outputs:
- affinity: float32 [3, 32, 64, 1024], P(None, 'sec', None, 'tile')
The draws below stay inside these ranges and needn't reach their ends.
All inputs are finite; a program needn't handle non-finite values.
Results may differ from the reference program's by a relative error of at most 0.00081.
Values may be sent and summed in bfloat16 or wider, within the bound.
No kernel may reach another device: no remote copies, remote signals or barrier semaphores. Data moves between devices by JAX's collectives and lax.ppermute only.
A program may use at most 128 MiB of HBM per device.

```python
import jax
import jax.numpy as jnp
from jax import lax

TY = 128
TX = 128
BLK = 16
C1 = 32
C3 = 64
AFF = 3
ZS = 32
XS = 2048
N_TILE = 16


def touch_ends(values, rng, smallest, largest):
    spot = [jax.random.randint(jax.random.fold_in(rng, axis), (), 0, length) for axis, length in enumerate(values.shape)]
    longest = values.shape.index(max(values.shape))
    next_to = spot[:longest] + [(spot[longest] + 1) % values.shape[longest]] + spot[longest + 1:]
    return values.at[tuple(spot)].set(smallest).at[tuple(next_to)].set(largest)


def level_of(stream_key, dims, split, least, top_value):
    def one(position, blocks):
        steps = jax.random.uniform(jax.random.fold_in(jax.random.fold_in(stream_key, 6), position), (blocks,), jnp.float32, least / len(split), top_value / len(split))
        return jnp.repeat(jnp.exp(steps), dims[position] // blocks).reshape((-1,) + (1,) * (len(dims) - position - 1))

    loudness = one(*split[0])
    for cut in split[1:]:
        loudness = loudness * one(*cut)
    return loudness


def centred(own_key, shape, spread, bound, cuts=(), kind=jnp.bfloat16):
    entries = jax.random.normal(own_key, shape, jnp.float32) * spread
    if len(cuts) > 0:
        entries = level_of(own_key, shape, cuts, -0.22, 0.18) * entries
    return jnp.clip(entries, min=-bound, max=bound).astype(kind)


def setup_inputs(seed: int = 0) -> dict:
    arg_keys = jax.random.split(jax.random.key(seed), 14)
    raw_sections = centred(arg_keys[0], (ZS, TY, XS), 1.0, 6.0, ((0, 16), (2, 16)))
    shift_cols = touch_ends(jax.random.randint(arg_keys[1], (ZS,), -(TX // BLK) * N_TILE // 2, (TX // BLK) * N_TILE // 2), jax.random.fold_in(arg_keys[1], 1), -(TX // BLK) * N_TILE // 2, ((TX // BLK) * N_TILE // 2) - 1).astype(jnp.int32)
    shift_rows = touch_ends(jax.random.randint(arg_keys[2], (ZS,), -((TY // BLK) // 4), (TY // BLK) // 4), jax.random.fold_in(arg_keys[2], 1), -((TY // BLK) // 4), ((TY // BLK) // 4) - 1).astype(jnp.int32)
    w_first = centred(arg_keys[3], (C1, 1, 3, 3), 9 ** -0.5, 2.0)
    b_first = centred(arg_keys[4], (C1,), 0.5, 3.0, (), jnp.float32)
    w_second = centred(arg_keys[5], (C1, C1, 3, 3), (9 * C1) ** -0.5, 0.375)
    b_second = centred(arg_keys[6], (C1,), 0.5, 3.0, (), jnp.float32)
    w_stride = centred(arg_keys[7], (C1, C1, 2, 2), (4 * C1) ** -0.5, 0.5)
    b_stride = centred(arg_keys[8], (C1,), 0.5, 3.0, (), jnp.float32)
    w_depth = centred(arg_keys[9], (C3, C1, 3, 3, 3), (27 * C1) ** -0.5, 0.21875)
    b_depth = centred(arg_keys[10], (C3,), 0.5, 3.0, (), jnp.float32)
    w_head = centred(arg_keys[11], (AFF, C3), C3 ** -0.5, 0.75, (), jnp.float32)
    b_head = centred(arg_keys[12], (AFF,), 1.0, 3.0, (), jnp.float32)
    return {"raw_sections": raw_sections, "shift_cols": shift_cols, "shift_rows": shift_rows, "w_first": w_first, "b_first": b_first, "w_second": w_second, "b_second": b_second, "w_stride": w_stride, "b_stride": b_stride, "w_depth": w_depth, "b_depth": b_depth, "w_head": w_head, "b_head": b_head}


def align_one(packed):
    section, offset_cols, offset_rows = packed
    padded = jnp.pad(section, ((TY, TY), (XS, XS)))
    start_row = (TY - BLK * offset_rows).astype(jnp.int32)
    start_col = (XS - BLK * offset_cols).astype(jnp.int32)
    return lax.dynamic_slice(padded, (start_row, start_col), (TY, XS))


def conv_plane(inputs, kernel, strides, padding):
    return lax.conv_general_dilated(inputs.astype(jnp.float32), kernel.astype(jnp.float32), strides, padding, precision=lax.Precision.HIGHEST)


def plane_layers(section, w_first, b_first, w_second, b_second, w_stride, b_stride):
    inputs = section[None, None]
    first = jax.nn.relu(conv_plane(inputs, w_first, (1, 1), ((1, 1), (1, 1))) + b_first[None, :, None, None]).astype(jnp.bfloat16)
    second = jax.nn.relu(conv_plane(first, w_second, (1, 1), ((1, 1), (1, 1))) + b_second[None, :, None, None]).astype(jnp.bfloat16)
    strided = jax.nn.relu(conv_plane(second, w_stride, (2, 2), "VALID") + b_stride[None, :, None, None]).astype(jnp.bfloat16)
    return strided[0]


def reference(raw_sections, shift_cols, shift_rows, w_first, b_first, w_second, b_second, w_stride, b_stride, w_depth, b_depth, w_head, b_head):
    aligned = lax.map(align_one, (raw_sections, shift_cols, shift_rows))
    strided = lax.map(lambda section: plane_layers(section, w_first, b_first, w_second, b_second, w_stride, b_stride), aligned)
    zpadded = jnp.pad(strided, ((1, 1), (0, 0), (0, 0), (0, 0)))

    def depth_one(index):
        window = lax.dynamic_slice_in_dim(zpadded, index, 3, 0)
        summed = jnp.zeros((C3, TY // 2, XS // 2), jnp.float32)
        for layer in range(3):
            summed = summed + conv_plane(window[layer][None], w_depth[:, :, layer], (1, 1), ((1, 1), (1, 1)))[0]
        deep = jax.nn.relu(summed + b_depth[:, None, None])
        logits = jnp.einsum("ko,oyx->kyx", w_head, deep, precision=lax.Precision.HIGHEST) + b_head[:, None, None]
        return jax.nn.sigmoid(logits)

    result = lax.map(depth_one, jnp.arange(ZS, dtype=jnp.int32))
    return jnp.transpose(result, (1, 0, 2, 3))
```

```python
import jax
import jax.numpy as jnp
from jax import lax
from jax.experimental import pallas as pl
from jax.experimental.pallas import tpu as pltpu
from jax.sharding import PartitionSpec as P

BLK = 16
TILES = 16
SECS = 16
HALO = 4
OFF = -1e30
BF = jnp.bfloat16
F32 = jnp.float32
SG = 11
VMEM = pltpu.VMEM
SMEM = pltpu.SMEM


def floor_lane(shape, dim):
    return lax.broadcasted_iota(jnp.int32, shape, dim)


def align_kernel(cols, rows, pos, gathered, out, tiles, lifted, sems):
    tile = pos[0]
    copies = []
    for z in range(2):
        start = 128 * tile - BLK * cols[z] - HALO
        first_tile = lax.shift_right_arithmetic(start, 7)
        for k in range(3):
            index = jnp.clip(first_tile + k, 0, TILES - 1)
            copy = pltpu.make_async_copy(gathered.at[index, z], tiles.at[z, k], sems.at[z, k])
            copy.start()
            copies.append(copy)
    lifted[0:32, :] = jnp.zeros((32, 256), F32)
    lifted[160:192, :] = jnp.zeros((32, 256), F32)
    lane = floor_lane((128, 128), 1)
    for z in range(2):
        start = 128 * tile - BLK * cols[z] - HALO
        first_tile = lax.shift_right_arithmetic(start, 7)
        offset = start - first_tile * 128
        turned = []
        for k in range(3):
            copies[3 * z + k].wait()
            inside = ((first_tile + k >= 0) & (first_tile + k < TILES)).astype(F32)
            value = tiles[z, k].astype(F32) * inside
            turned.append(pltpu.roll(value, 128 - offset, 1))
        low = jnp.where(lane < 128 - offset, turned[0], turned[1])
        high = jnp.where(lane < 128 - offset, turned[1], turned[2])
        low = jnp.where((tile == 0) & (lane < HALO), 0.0, low)
        high = jnp.where((tile == TILES - 1) & (lane >= HALO), 0.0, high)
        lifted[32:160, 0:128] = low
        lifted[32:160, 128:256] = high
        base = pl.multiple_of(32 - BLK * rows[z], BLK)
        out[z] = lifted[pl.ds(base, 128), :].astype(BF)


def align(gathered, cols, rows, pos):
    return pl.pallas_call(
        align_kernel,
        out_shape=jax.ShapeDtypeStruct((2, 128, 256), BF),
        in_specs=[pl.BlockSpec(memory_space=SMEM)] * 3 + [pl.BlockSpec(memory_space=pl.ANY)],
        out_specs=pl.BlockSpec(memory_space=VMEM),
        scratch_shapes=[
            pltpu.VMEM((2, 3, 128, 128), BF),
            pltpu.VMEM((192, 256), F32),
            pltpu.SemaphoreType.DMA((2, 3)),
        ],
        name="align",
    )(cols, rows, pos, gathered)


def front(tile, window, w1, bias1, w2, bias2, ws, biass, left, right, feats, strided):
    value = window.astype(F32)
    left[2:130, :] = value[:, 0:128]
    right[2:130, :] = value[:, 128:256]
    lane = floor_lane((32, 128), 1)
    patches = [None] * SG
    for j in range(8):
        low = left[pl.ds(j, 32, stride=4), :]
        high = right[pl.ds(j, 32, stride=4), :]
        ring = jnp.where(lane < 8, high, low)
        mine = (lane >= 16 * j) & (lane < 16 * j + 16)
        for g in range(SG):
            source = low if g < SG - 1 else ring
            shift = (16 * j - 12 * g) % 128
            turned = pltpu.roll(source, shift, 1) if shift else source
            patches[g] = turned if j == 0 else jnp.where(mine, turned, patches[g])
    patch = jnp.concatenate(patches, axis=0).astype(BF)
    for q in range(7):
        made = jnp.dot(patch, w1[:, 384 * q : 384 * (q + 1)], preferred_element_type=F32)
        made = jnp.maximum(made.reshape(SG, 32, 384) + bias1[...][None], 0.0)
        feats[:, 384 * q : 384 * (q + 1)] = made.reshape(SG * 32, 384).astype(BF)

    @pl.when(tile == 0)
    def _():
        feats[0:32, 0:576] = jnp.zeros((32, 576), BF)

    @pl.when(tile == TILES - 1)
    def _():
        feats[320:352, 2112:2688] = jnp.zeros((32, 576), BF)

    lane = floor_lane((SG, 32, 128), 2)
    row = floor_lane((SG, 32, 128), 1)
    from_above = (lane < 32) & (row > 0)
    from_below = (lane >= 96) & (row < 31)
    kept = (lane >= 32) & (lane < 96)
    for p in range(6):
        second = jnp.dot(
            feats[:, 384 * p : 384 * p + 768], w2[...], preferred_element_type=F32
        )
        second = jnp.maximum(second + bias2[...], 0.0).astype(BF)
        made = jnp.dot(second, ws[...], preferred_element_type=F32)
        made = jnp.maximum(made + biass[...], 0.0)
        down = pltpu.roll(made, 1, 0).reshape(SG, 32, 128)
        up = pltpu.roll(made, SG * 32 - 1, 0).reshape(SG, 32, 128)
        made = made.reshape(SG, 32, 128)
        made = jnp.where(kept, made, jnp.where(from_above, down, jnp.where(from_below, up, 0.0)))
        made = made.astype(BF)
        for g in range(SG):
            strided[p % 2, 3 * g + p // 2] = made[g]

    @pl.when(tile == 0)
    def _():
        strided[0, 0] = jnp.zeros((32, 128), BF)

    @pl.when(tile == TILES - 1)
    def _():
        strided[1, 32] = jnp.zeros((32, 128), BF)


def main_kernel(
    pos, window, w1, bias1, w2, bias2, ws, biass, wd, biasd, wh, bh, out, left, right, feats, strided
):
    tile = pos[0]
    sec = pos[1]
    for side in (left, right):
        side[0:2, :] = jnp.zeros((2, 128), F32)
        side[130:136, :] = jnp.zeros((6, 128), F32)

    def one(z, carry):
        front(
            tile, window[z], w1, bias1, w2, bias2, ws, biass, left, right, feats, strided.at[z]
        )
        return carry

    lax.fori_loop(0, 4, one, 0)

    @pl.when(sec == 0)
    def _():
        strided[0] = jnp.zeros((2, 33, 32, 128), BF)

    @pl.when(sec == SECS - 1)
    def _():
        strided[3] = jnp.zeros((2, 33, 32, 128), BF)

    lane = floor_lane((32, 128), 1)
    for z in range(2):
        spots = [jnp.zeros((32, 128), F32)] * 3
        for part in range(4):
            blocks = []
            for dz in range(3):
                for kx in range(4):
                    first = kx // 2 + 8 * part
                    blocks.append(strided[z + dz, kx % 2, first : first + 8].reshape(256, 128))
            patch = jnp.concatenate(blocks, axis=1)
            deep = jnp.dot(patch, wd[...], preferred_element_type=F32)
            deep = jnp.maximum(deep + biasd[...], 0.0)
            high = deep.astype(BF)
            low = (deep - high.astype(F32)).astype(BF)
            logits = jnp.dot(
                jnp.concatenate([high, low, high], axis=1), wh[...], preferred_element_type=F32
            )
            for step in range(8):
                m = 8 * part + step
                slab = logits[32 * step : 32 * step + 32]
                mine = (lane == 2 * m) | (lane == 2 * m + 1) | (lane == 64 + 2 * m) | (lane == 65 + 2 * m)
                for i in range(3):
                    shift = (2 * m - 2 * i) % 128
                    turned = pltpu.roll(slab, shift, 1) if shift else slab
                    spots[i] = jnp.where(mine, turned, spots[i])
        for i in range(3):
            for half in range(2):
                yp, k = divmod(2 * i + half, 3)
                value = spots[i] if half == 0 else pltpu.roll(spots[i], 64, 1)
                value = jax.nn.sigmoid(value[:, 0:64] + bh[k])
                out[k, z, pl.ds(yp, 32, stride=2), :] = value


def main(pos, window, *weights):
    return pl.pallas_call(
        main_kernel,
        out_shape=jax.ShapeDtypeStruct((3, 2, 64, 64), F32),
        in_specs=[pl.BlockSpec(memory_space=SMEM)]
        + [pl.BlockSpec(memory_space=VMEM)] * 10
        + [pl.BlockSpec(memory_space=SMEM)],
        out_specs=pl.BlockSpec(memory_space=VMEM),
        scratch_shapes=[
            pltpu.VMEM((136, 128), F32),
            pltpu.VMEM((136, 128), F32),
            pltpu.VMEM((SG * 32, 2688), BF),
            pltpu.VMEM((4, 2, 33, 32, 128), BF),
        ],
        compiler_params=pltpu.CompilerParams(vmem_limit_bytes=48 * 1024 * 1024),
        name="convs",
    )(pos, window, *weights)


def prepare_kernel(
    t1, t2, ts, td, th, b1, b2, bs, bd, w1, bias1, w2, bias2, ws, biass, wd, biasd, wh
):
    row = floor_lane((128, 384), 0)
    group = floor_lane((128, 384), 1) // 32
    dy = row // 16 - group % 6
    dx = row % 16 - group // 6
    base = jnp.zeros((128, 384), F32)
    for a in range(3):
        for b in range(3):
            spread = jnp.concatenate([t1[a, b : b + 1, :].astype(F32)] * 12, axis=1)
            base = jnp.where((dy == a) & (dx == b), spread, base)
    for q in range(7):
        turned = pltpu.roll(base, 2 * q, 0) if q else base
        w1[:, 384 * q : 384 * (q + 1)] = turned.astype(BF)
    lone = jnp.concatenate([b1[...]] * 12, axis=1)
    row = floor_lane((32, 384), 0)
    group = floor_lane((32, 384), 1) // 32 % 6
    outside = ((row == 0) & (group == 0)) | ((row == 31) & (group == 5))
    bias1[...] = jnp.where(outside, OFF, lone)
    bias2[...] = jnp.concatenate([b2[...]] * 8, axis=1)
    biass[...] = jnp.concatenate([bs[...]] * 4, axis=1)
    biasd[...] = jnp.concatenate([bd[...]] * 4, axis=1)

    lane = floor_lane((32, 128), 1)
    none = jnp.zeros((32, 128), F32)
    tiled = [
        [jnp.concatenate([t2[a, b].astype(F32)] * 4, axis=1) for b in range(3)] for a in range(3)
    ]
    for kx in range(4):
        for xp in range(2):
            b = kx - xp
            for j in range(6):
                made = none
                if 0 <= b < 3:
                    for a in range(3):
                        if 0 <= j - a < 4:
                            made = jnp.where(lane // 32 == j - a, tiled[a][b], made)
                start = 32 * (6 * kx + j)
                w2[start : start + 32, 128 * xp : 128 * xp + 128] = made.astype(BF)

    tiled = [
        [jnp.concatenate([ts[a, b].astype(F32)] * 4, axis=1) for b in range(2)] for a in range(2)
    ]
    for xp in range(2):
        for yp in range(4):
            mine = (lane // 32) % 2 == (1 if yp < 2 else 0)
            start = 32 * (4 * xp + yp)
            ws[start : start + 32, :] = jnp.where(mine, tiled[yp % 2][xp], 0.0).astype(BF)

    for dz in range(3):
        tiled = [
            [jnp.concatenate([td[dz, a, b].astype(F32)] * 2, axis=1) for b in range(3)]
            for a in range(3)
        ]
        for kx in range(4):
            for xp in range(2):
                b = kx - xp
                for slot in range(4):
                    made = none
                    if 0 <= b < 3:
                        low = tiled[slot][b] if slot < 3 else none
                        high = tiled[slot - 1][b] if slot > 0 else none
                        made = jnp.where(lane < 64, low, high)
                    start = 128 * (4 * dz + kx) + 32 * slot
                    wd[start : start + 32, 128 * xp : 128 * xp + 128] = made.astype(BF)

    lane = floor_lane((64, 128), 1)
    for xp in range(2):
        for yp in range(2):
            made = jnp.zeros((64, 128), F32)
            for k in range(3):
                c = 3 * yp + k
                made = jnp.where(lane == 64 * (c % 2) + 2 * (c // 2) + xp, th[:, k : k + 1], made)
            high = made.astype(BF)
            low = (made - high.astype(F32)).astype(BF)
            start = 64 * (2 * xp + yp)
            wh[start : start + 64, :] = high
            wh[256 + start : 256 + start + 64, :] = high
            wh[512 + start : 512 + start + 64, :] = low


def prepare(w_first, b_first, w_second, b_second, w_stride, b_stride, w_depth, b_depth, w_head):
    shape = jax.ShapeDtypeStruct
    return pl.pallas_call(
        prepare_kernel,
        out_shape=(
            shape((128, 2688), BF),
            shape((32, 384), F32),
            shape((768, 256), BF),
            shape((1, 256), F32),
            shape((256, 128), BF),
            shape((1, 128), F32),
            shape((1536, 256), BF),
            shape((1, 256), F32),
            shape((768, 128), BF),
        ),
        in_specs=[pl.BlockSpec(memory_space=VMEM)] * 9,
        out_specs=[pl.BlockSpec(memory_space=VMEM)] * 9,
        compiler_params=pltpu.CompilerParams(vmem_limit_bytes=32 * 1024 * 1024),
        cost_estimate=pl.CostEstimate(flops=1000000, bytes_accessed=4000000, transcendentals=0),
        name="prepare",
    )(
        jnp.transpose(w_first[:, 0], (1, 2, 0)),
        jnp.transpose(w_second, (2, 3, 1, 0)),
        jnp.transpose(w_stride, (2, 3, 1, 0)),
        jnp.transpose(w_depth, (2, 3, 4, 1, 0)),
        jnp.transpose(w_head),
        b_first[None],
        b_second[None],
        b_stride[None],
        b_depth[None],
    )


def local(
    raw_sections,
    shift_cols,
    shift_rows,
    w_first,
    b_first,
    w_second,
    b_second,
    w_stride,
    b_stride,
    w_depth,
    b_depth,
    w_head,
    b_head,
):
    pos = jnp.stack([lax.axis_index("tile"), lax.axis_index("sec")]).astype(jnp.int32)
    weights = prepare(
        w_first, b_first, w_second, b_second, w_stride, b_stride, w_depth, b_depth, w_head
    )
    copies = jnp.broadcast_to(raw_sections[None], (TILES,) + raw_sections.shape)
    gathered = lax.all_to_all(copies, "tile", 0, 0)
    window = align(gathered, shift_cols, shift_rows, pos)
    before = lax.ppermute(window[1:], "sec", [(i, i + 1) for i in range(SECS - 1)])
    after = lax.ppermute(window[:1], "sec", [(i + 1, i) for i in range(SECS - 1)])
    window = jnp.concatenate([before, window, after], axis=0)
    return main(pos, window, *weights, b_head)


def solution(mesh):
    in_specs = (P("sec", None, "tile"), P("sec"), P("sec")) + (P(),) * 10
    out_specs = P(None, "sec", None, "tile")
    return jax.shard_map(local, mesh=mesh, in_specs=in_specs, out_specs=out_specs, check_vma=False)
```

```python
import jax
import jax.numpy as jnp
from jax import lax
from jax.experimental import pallas as pl
from jax.experimental.pallas import tpu as pltpu
from jax.sharding import PartitionSpec as P

BLK = 16
TILES = 16
SECS = 16
HALO = 4
OFF = -1e30
BF = jnp.bfloat16
F32 = jnp.float32
SG = 11
VMEM = pltpu.VMEM
SMEM = pltpu.SMEM


def floor_lane(shape, dim):
    return lax.broadcasted_iota(jnp.int32, shape, dim)


def align_kernel(cols, rows, pos, gathered, out, tiles, lifted, sems):
    tile = pos[0]
    copies = []
    for z in range(2):
        start = 128 * tile - BLK * cols[z] - HALO
        first_tile = lax.shift_right_arithmetic(start, 7)
        for k in range(3):
            index = jnp.clip(first_tile + k, 0, TILES - 1)
            copy = pltpu.make_async_copy(gathered.at[index, z], tiles.at[z, k], sems.at[z, k])
            copy.start()
            copies.append(copy)
    lifted[0:32, :] = jnp.zeros((32, 256), F32)
    lifted[160:192, :] = jnp.zeros((32, 256), F32)
    lane = floor_lane((128, 128), 1)
    for z in range(2):
        start = 128 * tile - BLK * cols[z] - HALO
        first_tile = lax.shift_right_arithmetic(start, 7)
        offset = start - first_tile * 128
        turned = []
        for k in range(3):
            copies[3 * z + k].wait()
            inside = ((first_tile + k >= 0) & (first_tile + k < TILES)).astype(F32)
            value = tiles[z, k].astype(F32) * inside
            turned.append(pltpu.roll(value, 128 - offset, 1))
        low = jnp.where(lane < 128 - offset, turned[0], turned[1])
        high = jnp.where(lane < 128 - offset, turned[1], turned[2])
        low = jnp.where((tile == 0) & (lane < HALO), 0.0, low)
        high = jnp.where((tile == TILES - 1) & (lane >= HALO), 0.0, high)
        lifted[32:160, 0:128] = low
        lifted[32:160, 128:256] = high
        base = pl.multiple_of(32 - BLK * rows[z], BLK)
        out[z] = lifted[pl.ds(base, 128), :].astype(BF)


def align(gathered, cols, rows, pos):
    return pl.pallas_call(
        align_kernel,
        out_shape=jax.ShapeDtypeStruct((2, 128, 256), BF),
        in_specs=[pl.BlockSpec(memory_space=SMEM)] * 3 + [pl.BlockSpec(memory_space=pl.ANY)],
        out_specs=pl.BlockSpec(memory_space=VMEM),
        scratch_shapes=[
            pltpu.VMEM((2, 3, 128, 128), BF),
            pltpu.VMEM((192, 256), F32),
            pltpu.SemaphoreType.DMA((2, 3)),
        ],
        name="align",
    )(cols, rows, pos, gathered)


def front(tile, window, w1, bias1, w2, bias2, ws, biass, left, right, feats, second, strided):
    value = window.astype(F32)
    left[2:130, :] = value[:, 0:128]
    right[2:130, :] = value[:, 128:256]
    lane = floor_lane((32, 128), 1)
    patches = [None] * SG
    for j in range(8):
        low = left[pl.ds(j, 32, stride=4), :]
        high = right[pl.ds(j, 32, stride=4), :]
        ring = jnp.where(lane < 8, high, low)
        mine = (lane >= 16 * j) & (lane < 16 * j + 16)
        for g in range(SG):
            source = low if g < SG - 1 else ring
            shift = (16 * j - 12 * g) % 128
            turned = pltpu.roll(source, shift, 1) if shift else source
            patches[g] = turned if j == 0 else jnp.where(mine, turned, patches[g])
    patch = jnp.concatenate(patches, axis=0).astype(BF)
    for q in range(7):
        made = jnp.dot(patch, w1[:, 384 * q : 384 * (q + 1)], preferred_element_type=F32)
        made = jnp.maximum(made.reshape(SG, 32, 384) + bias1[...][None], 0.0)
        feats[:, 384 * q : 384 * (q + 1)] = made.reshape(SG * 32, 384).astype(BF)

    @pl.when(tile == 0)
    def _():
        feats[0:32, 0:576] = jnp.zeros((32, 576), BF)

    @pl.when(tile == TILES - 1)
    def _():
        feats[320:352, 2112:2688] = jnp.zeros((32, 576), BF)

    lane = floor_lane((SG, 32, 128), 2)
    row = floor_lane((SG, 32, 128), 1)
    from_above = (lane < 32) & (row > 0)
    from_below = (lane >= 96) & (row < 31)
    kept = (lane >= 32) & (lane < 96)
    for p in range(6):
        made = jnp.dot(
            feats[:, 384 * p : 384 * p + 768], w2[...], preferred_element_type=F32
        )
        second[p] = jnp.maximum(made + bias2[...], 0.0).astype(BF)
    for p in range(6):
        made = jnp.dot(second[p], ws[...], preferred_element_type=F32)
        made = jnp.maximum(made + biass[...], 0.0)
        down = pltpu.roll(made, 1, 0).reshape(SG, 32, 128)
        up = pltpu.roll(made, SG * 32 - 1, 0).reshape(SG, 32, 128)
        made = made.reshape(SG, 32, 128)
        made = jnp.where(kept, made, jnp.where(from_above, down, jnp.where(from_below, up, 0.0)))
        made = made.astype(BF)
        for g in range(SG):
            strided[p % 2, 3 * g + p // 2] = made[g]

    @pl.when(tile == 0)
    def _():
        strided[0, 0] = jnp.zeros((32, 128), BF)

    @pl.when(tile == TILES - 1)
    def _():
        strided[1, 32] = jnp.zeros((32, 128), BF)


def clear_edges(left, right):
    for side in (left, right):
        side[0:2, :] = jnp.zeros((2, 128), F32)
        side[130:136, :] = jnp.zeros((6, 128), F32)


def own_kernel(pos, window, w1, bias1, w2, bias2, ws, biass, out, left, right, feats, second):
    clear_edges(left, right)

    def one(z, carry):
        front(
            pos[0], window[z], w1, bias1, w2, bias2, ws, biass, left, right, feats, second, out.at[z]
        )
        return carry

    lax.fori_loop(0, 2, one, 0)


SCRATCH = [
    pltpu.VMEM((136, 128), F32),
    pltpu.VMEM((136, 128), F32),
    pltpu.VMEM((SG * 32, 2688), BF),
    pltpu.VMEM((6, SG * 32, 256), BF),
]


def own(pos, window, *weights):
    return pl.pallas_call(
        own_kernel,
        out_shape=jax.ShapeDtypeStruct((2, 2, 33, 32, 128), BF),
        in_specs=[pl.BlockSpec(memory_space=SMEM)] + [pl.BlockSpec(memory_space=VMEM)] * 7,
        out_specs=pl.BlockSpec(memory_space=VMEM),
        scratch_shapes=SCRATCH,
        compiler_params=pltpu.CompilerParams(vmem_limit_bytes=24 * 1024 * 1024),
        cost_estimate=pl.CostEstimate(flops=4000000000, bytes_accessed=4000000, transcendentals=0),
        name="own",
    )(pos, window, *weights)


def main_kernel(
    pos, before, after, middle, w1, bias1, w2, bias2, ws, biass, wd, biasd, wh, bh, out,
    left, right, feats, second, outer, deeps,
):
    tile = pos[0]
    sec = pos[1]
    clear_edges(left, right)

    @pl.when(sec == 0)
    def _():
        outer[0] = jnp.zeros((2, 33, 32, 128), BF)

    @pl.when(sec == SECS - 1)
    def _():
        outer[1] = jnp.zeros((2, 33, 32, 128), BF)

    def one(z, carry):
        @pl.when((sec > 0) | (z > 0))
        def _():
            @pl.when((sec < SECS - 1) | (z < 1))
            def _():
                window = jnp.where(z == 0, before[0], after[0])
                front(
                    tile, window, w1, bias1, w2, bias2, ws, biass, left, right, feats, second, outer.at[z]
                )

        return carry

    lax.fori_loop(0, 2, one, 0)
    for z in range(2):
        for part in range(4):
            blocks = []
            for dz in range(3):
                source = (outer.at[0], middle.at[0], middle.at[1], outer.at[1])[z + dz]
                for kx in range(4):
                    first = kx // 2 + 8 * part
                    blocks.append(source[kx % 2, first : first + 8].reshape(256, 128))
            patch = jnp.concatenate(blocks, axis=1)
            deep = jnp.dot(patch, wd[...], preferred_element_type=F32)
            deep = jnp.maximum(deep + biasd[...], 0.0)
            high = deep.astype(BF)
            deeps[z, part, :, 0:256] = high
            deeps[z, part, :, 256:512] = (deep - high.astype(F32)).astype(BF)
            deeps[z, part, :, 512:768] = high
    lane = floor_lane((32, 128), 1)
    for z in range(2):
        spots = [jnp.zeros((32, 128), F32)] * 3
        for part in range(4):
            logits = jnp.dot(deeps[z, part], wh[...], preferred_element_type=F32)
            for step in range(8):
                m = 8 * part + step
                slab = logits[32 * step : 32 * step + 32]
                mine = (lane == 2 * m) | (lane == 2 * m + 1) | (lane == 64 + 2 * m) | (lane == 65 + 2 * m)
                for i in range(3):
                    shift = (2 * m - 2 * i) % 128
                    turned = pltpu.roll(slab, shift, 1) if shift else slab
                    spots[i] = jnp.where(mine, turned, spots[i])
        for i in range(3):
            for half in range(2):
                yp, k = divmod(2 * i + half, 3)
                value = spots[i] if half == 0 else pltpu.roll(spots[i], 64, 1)
                value = jax.nn.sigmoid(value[:, 0:64] + bh[k])
                out[k, z, pl.ds(yp, 32, stride=2), :] = value


def main(pos, before, after, middle, *weights):
    return pl.pallas_call(
        main_kernel,
        out_shape=jax.ShapeDtypeStruct((3, 2, 64, 64), F32),
        in_specs=[pl.BlockSpec(memory_space=SMEM)]
        + [pl.BlockSpec(memory_space=VMEM)] * 12
        + [pl.BlockSpec(memory_space=SMEM)],
        out_specs=pl.BlockSpec(memory_space=VMEM),
        scratch_shapes=SCRATCH
        + [pltpu.VMEM((2, 2, 33, 32, 128), BF), pltpu.VMEM((2, 4, 256, 768), BF)],
        compiler_params=pltpu.CompilerParams(vmem_limit_bytes=32 * 1024 * 1024),
        name="convs",
    )(pos, before, after, middle, *weights)


def prepare_kernel(
    t1, t2, ts, td, th, b1, b2, bs, bd, w1, bias1, w2, bias2, ws, biass, wd, biasd, wh
):
    row = floor_lane((128, 384), 0)
    group = floor_lane((128, 384), 1) // 32
    dy = row // 16 - group % 6
    dx = row % 16 - group // 6
    base = jnp.zeros((128, 384), F32)
    for a in range(3):
        for b in range(3):
            spread = jnp.concatenate([t1[a, b : b + 1, :].astype(F32)] * 12, axis=1)
            base = jnp.where((dy == a) & (dx == b), spread, base)
    for q in range(7):
        turned = pltpu.roll(base, 2 * q, 0) if q else base
        w1[:, 384 * q : 384 * (q + 1)] = turned.astype(BF)
    lone = jnp.concatenate([b1[...]] * 12, axis=1)
    row = floor_lane((32, 384), 0)
    group = floor_lane((32, 384), 1) // 32 % 6
    outside = ((row == 0) & (group == 0)) | ((row == 31) & (group == 5))
    bias1[...] = jnp.where(outside, OFF, lone)
    bias2[...] = jnp.concatenate([b2[...]] * 8, axis=1)
    biass[...] = jnp.concatenate([bs[...]] * 4, axis=1)
    biasd[...] = jnp.concatenate([bd[...]] * 4, axis=1)

    lane = floor_lane((32, 128), 1)
    none = jnp.zeros((32, 128), F32)
    tiled = [
        [jnp.concatenate([t2[a, b].astype(F32)] * 4, axis=1) for b in range(3)] for a in range(3)
    ]
    for kx in range(4):
        for xp in range(2):
            b = kx - xp
            for j in range(6):
                made = none
                if 0 <= b < 3:
                    for a in range(3):
                        if 0 <= j - a < 4:
                            made = jnp.where(lane // 32 == j - a, tiled[a][b], made)
                start = 32 * (6 * kx + j)
                w2[start : start + 32, 128 * xp : 128 * xp + 128] = made.astype(BF)

    tiled = [
        [jnp.concatenate([ts[a, b].astype(F32)] * 4, axis=1) for b in range(2)] for a in range(2)
    ]
    for xp in range(2):
        for yp in range(4):
            mine = (lane // 32) % 2 == (1 if yp < 2 else 0)
            start = 32 * (4 * xp + yp)
            ws[start : start + 32, :] = jnp.where(mine, tiled[yp % 2][xp], 0.0).astype(BF)

    for dz in range(3):
        tiled = [
            [jnp.concatenate([td[dz, a, b].astype(F32)] * 2, axis=1) for b in range(3)]
            for a in range(3)
        ]
        for kx in range(4):
            for xp in range(2):
                b = kx - xp
                for slot in range(4):
                    made = none
                    if 0 <= b < 3:
                        low = tiled[slot][b] if slot < 3 else none
                        high = tiled[slot - 1][b] if slot > 0 else none
                        made = jnp.where(lane < 64, low, high)
                    start = 128 * (4 * dz + kx) + 32 * slot
                    wd[start : start + 32, 128 * xp : 128 * xp + 128] = made.astype(BF)

    lane = floor_lane((64, 128), 1)
    for xp in range(2):
        for yp in range(2):
            made = jnp.zeros((64, 128), F32)
            for k in range(3):
                c = 3 * yp + k
                made = jnp.where(lane == 64 * (c % 2) + 2 * (c // 2) + xp, th[:, k : k + 1], made)
            high = made.astype(BF)
            low = (made - high.astype(F32)).astype(BF)
            start = 64 * (2 * xp + yp)
            wh[start : start + 64, :] = high
            wh[256 + start : 256 + start + 64, :] = high
            wh[512 + start : 512 + start + 64, :] = low


def prepare(w_first, b_first, w_second, b_second, w_stride, b_stride, w_depth, b_depth, w_head):
    shape = jax.ShapeDtypeStruct
    return pl.pallas_call(
        prepare_kernel,
        out_shape=(
            shape((128, 2688), BF),
            shape((32, 384), F32),
            shape((768, 256), BF),
            shape((1, 256), F32),
            shape((256, 128), BF),
            shape((1, 128), F32),
            shape((1536, 256), BF),
            shape((1, 256), F32),
            shape((768, 128), BF),
        ),
        in_specs=[pl.BlockSpec(memory_space=VMEM)] * 9,
        out_specs=[pl.BlockSpec(memory_space=VMEM)] * 9,
        compiler_params=pltpu.CompilerParams(vmem_limit_bytes=32 * 1024 * 1024),
        cost_estimate=pl.CostEstimate(flops=1000000, bytes_accessed=4000000, transcendentals=0),
        name="prepare",
    )(
        jnp.transpose(w_first[:, 0], (1, 2, 0)),
        jnp.transpose(w_second, (2, 3, 1, 0)),
        jnp.transpose(w_stride, (2, 3, 1, 0)),
        jnp.transpose(w_depth, (2, 3, 4, 1, 0)),
        jnp.transpose(w_head),
        b_first[None],
        b_second[None],
        b_stride[None],
        b_depth[None],
    )


def local(
    raw_sections,
    shift_cols,
    shift_rows,
    w_first,
    b_first,
    w_second,
    b_second,
    w_stride,
    b_stride,
    w_depth,
    b_depth,
    w_head,
    b_head,
):
    pos = jnp.stack([lax.axis_index("tile"), lax.axis_index("sec")]).astype(jnp.int32)
    weights = prepare(
        w_first, b_first, w_second, b_second, w_stride, b_stride, w_depth, b_depth, w_head
    )
    copies = jnp.broadcast_to(raw_sections[None], (TILES,) + raw_sections.shape)
    gathered = lax.all_to_all(copies, "tile", 0, 0)
    window = align(gathered, shift_cols, shift_rows, pos)
    before = lax.ppermute(window[1:], "sec", [(i, i + 1) for i in range(SECS - 1)])
    after = lax.ppermute(window[:1], "sec", [(i + 1, i) for i in range(SECS - 1)])
    middle = own(pos, window, *weights[:6])
    return main(pos, before, after, middle, *weights, b_head)


def solution(mesh):
    in_specs = (P("sec", None, "tile"), P("sec"), P("sec")) + (P(),) * 10
    out_specs = P(None, "sec", None, "tile")
    return jax.shard_map(local, mesh=mesh, in_specs=in_specs, out_specs=out_specs, check_vma=False)
```

```python
import jax
import jax.numpy as jnp
from jax import lax
from jax.experimental import pallas as pl
from jax.experimental.pallas import tpu as pltpu
from jax.sharding import PartitionSpec as P

BLK = 16
TILES = 16
SECS = 16
HALO = 4
OFF = -1e30
BF = jnp.bfloat16
F32 = jnp.float32
SG = 11
VMEM = pltpu.VMEM
SMEM = pltpu.SMEM


def floor_lane(shape, dim):
    return lax.broadcasted_iota(jnp.int32, shape, dim)


def first_tile_of(tile, shift):
    start = 128 * tile - BLK * shift - HALO
    first = lax.shift_right_arithmetic(start, 7)
    return first, start - first * 128


def chosen(sources, index, z):
    value = sources[0][z]
    for k in range(1, len(sources)):
        value = jnp.where(index == k, sources[k][z], value)
    return value


def pick_kernel(spot, mine, one, two, three, keep, send_1, send_2, send_3):
    sources = (mine, one, two, three)
    tile = spot[4]
    place = tile & 3
    for z in range(2):
        for step, out in enumerate((keep, send_1, send_2, send_3)):
            goal = (tile - place) + ((place + step) & 3)
            first, _ = first_tile_of(goal, spot[z])
            wanted = first + ((place - first) & 3)
            index = (lax.shift_right_arithmetic(tile, 2) - lax.shift_right_arithmetic(wanted, 2)) & 3
            out[z] = chosen(sources, index, z)


def pick(spot, *sources):
    return pl.pallas_call(
        pick_kernel,
        out_shape=[jax.ShapeDtypeStruct((2, 128, 128), BF)] * 4,
        in_specs=[pl.BlockSpec(memory_space=SMEM)] + [pl.BlockSpec(memory_space=VMEM)] * 4,
        out_specs=[pl.BlockSpec(memory_space=VMEM)] * 4,
        compiler_params=pltpu.CompilerParams(vmem_limit_bytes=8 * 1024 * 1024),
        cost_estimate=pl.CostEstimate(flops=0, bytes_accessed=16000000, transcendentals=0),
        name="pick",
    )(spot, *sources)


def align_kernel(spot, keep, one, two, three, low_section, high_section, lifted):
    sources = (keep, one, two, three)
    tile = spot[4]
    lifted[0:32, :] = jnp.zeros((32, 256), F32)
    lifted[160:192, :] = jnp.zeros((32, 256), F32)
    lane = floor_lane((128, 128), 1)
    for z, out in enumerate((low_section, high_section)):
        first, offset = first_tile_of(tile, spot[z])
        turned = []
        for k in range(3):
            inside = ((first + k >= 0) & (first + k < TILES)).astype(F32)
            value = chosen(sources, (tile - first - k) & 3, z).astype(F32) * inside
            turned.append(pltpu.roll(value, 128 - offset, 1))
        low = jnp.where(lane < 128 - offset, turned[0], turned[1])
        high = jnp.where(lane < 128 - offset, turned[1], turned[2])
        low = jnp.where((tile == 0) & (lane < HALO), 0.0, low)
        high = jnp.where((tile == TILES - 1) & (lane >= HALO), 0.0, high)
        lifted[32:160, 0:128] = low
        lifted[32:160, 128:256] = high
        base = pl.multiple_of(32 - BLK * spot[2 + z], BLK)
        out[0] = lifted[pl.ds(base, 128), :].astype(BF)


def align(spot, *sources):
    return pl.pallas_call(
        align_kernel,
        out_shape=[jax.ShapeDtypeStruct((1, 128, 256), BF)] * 2,
        in_specs=[pl.BlockSpec(memory_space=SMEM)] + [pl.BlockSpec(memory_space=VMEM)] * 4,
        out_specs=[pl.BlockSpec(memory_space=VMEM)] * 2,
        scratch_shapes=[pltpu.VMEM((192, 256), F32)],
        compiler_params=pltpu.CompilerParams(vmem_limit_bytes=8 * 1024 * 1024),
        cost_estimate=pl.CostEstimate(flops=0, bytes_accessed=4000000, transcendentals=0),
        name="align",
    )(spot, *sources)


def front(tile, window, w1, bias1, w2, bias2, ws, biass, left, right, feats, second, strided):
    value = window.astype(F32)
    left[2:130, :] = value[:, 0:128]
    right[2:130, :] = value[:, 128:256]
    lane = floor_lane((32, 128), 1)
    patches = [None] * SG
    for j in range(8):
        low = left[pl.ds(j, 32, stride=4), :]
        high = right[pl.ds(j, 32, stride=4), :]
        ring = jnp.where(lane < 8, high, low)
        mine = (lane >= 16 * j) & (lane < 16 * j + 16)
        for g in range(SG):
            source = low if g < SG - 1 else ring
            shift = (16 * j - 12 * g) % 128
            turned = pltpu.roll(source, shift, 1) if shift else source
            patches[g] = turned if j == 0 else jnp.where(mine, turned, patches[g])
    patch = jnp.concatenate(patches, axis=0).astype(BF)
    for q in range(7):
        made = jnp.dot(patch, w1[:, 384 * q : 384 * (q + 1)], preferred_element_type=F32)
        made = jnp.maximum(made.reshape(SG, 32, 384) + bias1[...][None], 0.0)
        feats[:, 384 * q : 384 * (q + 1)] = made.reshape(SG * 32, 384).astype(BF)

    @pl.when(tile == 0)
    def _():
        feats[0:32, 0:576] = jnp.zeros((32, 576), BF)

    @pl.when(tile == TILES - 1)
    def _():
        feats[320:352, 2112:2688] = jnp.zeros((32, 576), BF)

    lane = floor_lane((SG, 32, 128), 2)
    row = floor_lane((SG, 32, 128), 1)
    from_above = (lane < 32) & (row > 0)
    from_below = (lane >= 96) & (row < 31)
    kept = (lane >= 32) & (lane < 96)
    for p in range(6):
        made = jnp.dot(
            feats[:, 384 * p : 384 * p + 768], w2[...], preferred_element_type=F32
        )
        second[p] = jnp.maximum(made + bias2[...], 0.0).astype(BF)
    for p in range(6):
        made = jnp.dot(second[p], ws[...], preferred_element_type=F32)
        made = jnp.maximum(made + biass[...], 0.0)
        down = pltpu.roll(made, 1, 0).reshape(SG, 32, 128)
        up = pltpu.roll(made, SG * 32 - 1, 0).reshape(SG, 32, 128)
        made = made.reshape(SG, 32, 128)
        made = jnp.where(kept, made, jnp.where(from_above, down, jnp.where(from_below, up, 0.0)))
        made = made.astype(BF)
        for g in range(SG):
            strided[p % 2, 3 * g + p // 2] = made[g]

    @pl.when(tile == 0)
    def _():
        strided[0, 0] = jnp.zeros((32, 128), BF)

    @pl.when(tile == TILES - 1)
    def _():
        strided[1, 32] = jnp.zeros((32, 128), BF)


def clear_edges(left, right):
    for side in (left, right):
        side[0:2, :] = jnp.zeros((2, 128), F32)
        side[130:136, :] = jnp.zeros((6, 128), F32)


def own_kernel(spot, low_section, high_section, w1, bias1, w2, bias2, ws, biass, out, left, right, feats, second):
    clear_edges(left, right)

    def one(z, carry):
        window = jnp.where(z == 0, low_section[0], high_section[0])
        front(
            spot[4], window, w1, bias1, w2, bias2, ws, biass, left, right, feats, second, out.at[z]
        )
        return carry

    lax.fori_loop(0, 2, one, 0)


SCRATCH = [
    pltpu.VMEM((136, 128), F32),
    pltpu.VMEM((136, 128), F32),
    pltpu.VMEM((SG * 32, 2688), BF),
    pltpu.VMEM((6, SG * 32, 256), BF),
]


def own(spot, low_section, high_section, *weights):
    return pl.pallas_call(
        own_kernel,
        out_shape=jax.ShapeDtypeStruct((2, 2, 33, 32, 128), BF),
        in_specs=[pl.BlockSpec(memory_space=SMEM)] + [pl.BlockSpec(memory_space=VMEM)] * 8,
        out_specs=pl.BlockSpec(memory_space=VMEM),
        scratch_shapes=SCRATCH,
        compiler_params=pltpu.CompilerParams(vmem_limit_bytes=24 * 1024 * 1024),
        cost_estimate=pl.CostEstimate(flops=4000000000, bytes_accessed=4000000, transcendentals=0),
        name="own",
    )(spot, low_section, high_section, *weights)


def main_kernel(
    spot, before, after, middle, w1, bias1, w2, bias2, ws, biass, wd, biasd, wh, bh, out,
    left, right, feats, second, outer, deeps,
):
    tile = spot[4]
    sec = spot[5]
    clear_edges(left, right)

    @pl.when(sec == 0)
    def _():
        outer[0] = jnp.zeros((2, 33, 32, 128), BF)

    @pl.when(sec == SECS - 1)
    def _():
        outer[1] = jnp.zeros((2, 33, 32, 128), BF)

    def one(z, carry):
        @pl.when((sec > 0) | (z > 0))
        def _():
            @pl.when((sec < SECS - 1) | (z < 1))
            def _():
                window = jnp.where(z == 0, before[0], after[0])
                front(
                    tile, window, w1, bias1, w2, bias2, ws, biass, left, right, feats, second, outer.at[z]
                )

        return carry

    lax.fori_loop(0, 2, one, 0)
    for z in range(2):
        for part in range(4):
            blocks = []
            for dz in range(3):
                source = (outer.at[0], middle.at[0], middle.at[1], outer.at[1])[z + dz]
                for kx in range(4):
                    first = kx // 2 + 8 * part
                    blocks.append(source[kx % 2, first : first + 8].reshape(256, 128))
            patch = jnp.concatenate(blocks, axis=1)
            deep = jnp.dot(patch, wd[...], preferred_element_type=F32)
            deep = jnp.maximum(deep + biasd[...], 0.0)
            high = deep.astype(BF)
            deeps[z, part, :, 0:256] = high
            deeps[z, part, :, 256:512] = (deep - high.astype(F32)).astype(BF)
            deeps[z, part, :, 512:768] = high
    lane = floor_lane((32, 128), 1)
    for z in range(2):
        spots = [jnp.zeros((32, 128), F32)] * 3
        for part in range(4):
            logits = jnp.dot(deeps[z, part], wh[...], preferred_element_type=F32)
            for step in range(8):
                m = 8 * part + step
                slab = logits[32 * step : 32 * step + 32]
                mine = (lane == 2 * m) | (lane == 2 * m + 1) | (lane == 64 + 2 * m) | (lane == 65 + 2 * m)
                for i in range(3):
                    shift = (2 * m - 2 * i) % 128
                    turned = pltpu.roll(slab, shift, 1) if shift else slab
                    spots[i] = jnp.where(mine, turned, spots[i])
        for i in range(3):
            for half in range(2):
                yp, k = divmod(2 * i + half, 3)
                value = spots[i] if half == 0 else pltpu.roll(spots[i], 64, 1)
                value = jax.nn.sigmoid(value[:, 0:64] + bh[k])
                out[k, z, pl.ds(yp, 32, stride=2), :] = value


def main(spot, before, after, middle, *weights):
    return pl.pallas_call(
        main_kernel,
        out_shape=jax.ShapeDtypeStruct((3, 2, 64, 64), F32),
        in_specs=[pl.BlockSpec(memory_space=SMEM)]
        + [pl.BlockSpec(memory_space=VMEM)] * 12
        + [pl.BlockSpec(memory_space=SMEM)],
        out_specs=pl.BlockSpec(memory_space=VMEM),
        scratch_shapes=SCRATCH
        + [pltpu.VMEM((2, 2, 33, 32, 128), BF), pltpu.VMEM((2, 4, 256, 768), BF)],
        compiler_params=pltpu.CompilerParams(vmem_limit_bytes=32 * 1024 * 1024),
        name="convs",
    )(spot, before, after, middle, *weights)


def prepare_kernel(*refs):
    small, t2, ts, td = refs[:4]
    w1, bias1, w2, bias2, ws, biass, wd, biasd, wh = refs[4:]
    b1, b2, bs = (small[12 + i : 13 + i, 0:32] for i in range(3))
    bd = small[15:16, :]
    row = floor_lane((128, 384), 0)
    group = floor_lane((128, 384), 1) // 32
    dy = row // 16 - group % 6
    dx = row % 16 - group // 6
    base = jnp.zeros((128, 384), F32)
    for a in range(3):
        for b in range(3):
            spread = jnp.concatenate([small[3 * a + b : 3 * a + b + 1, 0:32]] * 12, axis=1)
            base = jnp.where((dy == a) & (dx == b), spread, base)
    for q in range(7):
        turned = pltpu.roll(base, 2 * q, 0) if q else base
        w1[:, 384 * q : 384 * (q + 1)] = turned.astype(BF)
    lone = jnp.concatenate([b1] * 12, axis=1)
    row = floor_lane((32, 384), 0)
    group = floor_lane((32, 384), 1) // 32 % 6
    outside = ((row == 0) & (group == 0)) | ((row == 31) & (group == 5))
    bias1[...] = jnp.where(outside, OFF, lone)
    bias2[...] = jnp.concatenate([b2] * 8, axis=1)
    biass[...] = jnp.concatenate([bs] * 4, axis=1)
    biasd[...] = jnp.concatenate([bd] * 4, axis=1)

    lane = floor_lane((32, 128), 1)
    none = jnp.zeros((32, 128), F32)
    tiled = [
        [jnp.concatenate([t2[a, b].astype(F32).T] * 4, axis=1) for b in range(3)] for a in range(3)
    ]
    for kx in range(4):
        for xp in range(2):
            b = kx - xp
            for j in range(6):
                made = none
                if 0 <= b < 3:
                    for a in range(3):
                        if 0 <= j - a < 4:
                            made = jnp.where(lane // 32 == j - a, tiled[a][b], made)
                start = 32 * (6 * kx + j)
                w2[start : start + 32, 128 * xp : 128 * xp + 128] = made.astype(BF)

    tiled = [
        [jnp.concatenate([ts[a, b].astype(F32)] * 4, axis=1) for b in range(2)] for a in range(2)
    ]
    for xp in range(2):
        for yp in range(4):
            mine = (lane // 32) % 2 == (1 if yp < 2 else 0)
            start = 32 * (4 * xp + yp)
            ws[start : start + 32, :] = jnp.where(mine, tiled[yp % 2][xp], 0.0).astype(BF)

    for dz in range(3):
        tiled = [
            [jnp.concatenate([td[dz, a, b].astype(F32)] * 2, axis=1) for b in range(3)]
            for a in range(3)
        ]
        for kx in range(4):
            for xp in range(2):
                b = kx - xp
                for slot in range(4):
                    made = none
                    if 0 <= b < 3:
                        low = tiled[slot][b] if slot < 3 else none
                        high = tiled[slot - 1][b] if slot > 0 else none
                        made = jnp.where(lane < 64, low, high)
                    start = 128 * (4 * dz + kx) + 32 * slot
                    wd[start : start + 32, 128 * xp : 128 * xp + 128] = made.astype(BF)

    lane = floor_lane((64, 128), 1)
    heads = jnp.concatenate([small[9:12, :], jnp.zeros((5, 64), F32)], axis=0).T
    for xp in range(2):
        for yp in range(2):
            made = jnp.zeros((64, 128), F32)
            for k in range(3):
                c = 3 * yp + k
                made = jnp.where(lane == 64 * (c % 2) + 2 * (c // 2) + xp, heads[:, k : k + 1], made)
            high = made.astype(BF)
            low = (made - high.astype(F32)).astype(BF)
            start = 64 * (2 * xp + yp)
            wh[start : start + 64, :] = high
            wh[256 + start : 256 + start + 64, :] = high
            wh[512 + start : 512 + start + 64, :] = low


def prepare(w_first, b_first, w_second, b_second, w_stride, b_stride, w_depth, b_depth, w_head):
    shape = jax.ShapeDtypeStruct
    lines = (
        jnp.transpose(w_first[:, 0], (1, 2, 0)).reshape(9, 32).astype(F32),
        w_head,
        b_first[None],
        b_second[None],
        b_stride[None],
        b_depth[None],
    )
    small = jnp.concatenate([jnp.pad(v, ((0, 0), (0, 64 - v.shape[1]))) for v in lines], axis=0)
    given = (
        small,
        jnp.transpose(w_second, (2, 3, 0, 1)),
        jnp.transpose(w_stride, (2, 3, 1, 0)),
        jnp.transpose(w_depth, (2, 3, 4, 1, 0)),
    )
    return pl.pallas_call(
        prepare_kernel,
        out_shape=(
            shape((128, 2688), BF),
            shape((32, 384), F32),
            shape((768, 256), BF),
            shape((1, 256), F32),
            shape((256, 128), BF),
            shape((1, 128), F32),
            shape((1536, 256), BF),
            shape((1, 256), F32),
            shape((768, 128), BF),
        ),
        in_specs=[pl.BlockSpec(memory_space=VMEM)] * 4,
        out_specs=[pl.BlockSpec(memory_space=VMEM)] * 9,
        compiler_params=pltpu.CompilerParams(vmem_limit_bytes=16 * 1024 * 1024),
        cost_estimate=pl.CostEstimate(flops=1000000, bytes_accessed=4000000, transcendentals=0),
        name="prepare",
    )(*given)


def local(
    raw_sections,
    shift_cols,
    shift_rows,
    w_first,
    b_first,
    w_second,
    b_second,
    w_stride,
    b_stride,
    w_depth,
    b_depth,
    w_head,
    b_head,
):
    place = jnp.stack([lax.axis_index("tile"), lax.axis_index("sec")]).astype(jnp.int32)
    spot = jnp.concatenate([shift_cols, shift_rows, place])
    weights = prepare(
        w_first, b_first, w_second, b_second, w_stride, b_stride, w_depth, b_depth, w_head
    )
    columns = [
        lax.ppermute(raw_sections, "tile", [(i, (i + 4 * k) % TILES) for i in range(TILES)])
        for k in (1, 2, 3)
    ]
    keep, *sends = pick(spot, raw_sections, *columns)
    pieces = [
        lax.ppermute(send, "tile", [(i, i - i % 4 + (i + k) % 4) for i in range(TILES)])
        for k, send in zip((1, 2, 3), sends)
    ]
    low_section, high_section = align(spot, keep, *pieces)
    before = lax.ppermute(high_section, "sec", [(i, i + 1) for i in range(SECS - 1)])
    after = lax.ppermute(low_section, "sec", [(i + 1, i) for i in range(SECS - 1)])
    middle = own(spot, low_section, high_section, *weights[:6])
    return main(spot, before, after, middle, *weights, b_head)


def solution(mesh):
    in_specs = (P("sec", None, "tile"), P("sec"), P("sec")) + (P(),) * 10
    out_specs = P(None, "sec", None, "tile")
    return jax.shard_map(local, mesh=mesh, in_specs=in_specs, out_specs=out_specs, check_vma=False)
```

```python
import jax
import jax.numpy as jnp
from jax import lax
from jax.experimental import pallas as pl
from jax.experimental.pallas import tpu as pltpu
from jax.sharding import PartitionSpec as P

BLK = 16
TILES = 16
SECS = 16
HALO = 4
OFF = -1e30
BF = jnp.bfloat16
F32 = jnp.float32
SG = 11
VMEM = pltpu.VMEM
SMEM = pltpu.SMEM


COLS, ROWS, TILE, SEC = 0, 2, 4, 5


def floor_lane(shape, dim):
    return lax.broadcasted_iota(jnp.int32, shape, dim)


def first_tile_of(tile, shift):
    start = 128 * tile - BLK * shift - HALO
    first = lax.shift_right_arithmetic(start, 7)
    return first, start - first * 128


def chosen(sources, index, z):
    value = sources[0][z]
    for k in range(1, len(sources)):
        value = jnp.where(index == k, sources[k][z], value)
    return value


def stage_kernel(given, out):
    out[...] = given[...]


def stage(raw):
    return pl.pallas_call(
        stage_kernel,
        out_shape=jax.ShapeDtypeStruct(raw.shape, raw.dtype),
        in_specs=[pl.BlockSpec(memory_space=VMEM)],
        out_specs=pl.BlockSpec(memory_space=VMEM),
        compiler_params=pltpu.CompilerParams(vmem_limit_bytes=8 * 1024 * 1024),
        cost_estimate=pl.CostEstimate(flops=0, bytes_accessed=4000000, transcendentals=0),
        name="stage",
    )(raw)


def pick_kernel(spot, mine, one, two, three, keep, send_1, send_2, send_3):
    sources = (mine, one, two, three)
    tile = spot[TILE]
    place = tile & 3
    for z in range(2):
        for step, out in enumerate((keep, send_1, send_2, send_3)):
            goal = tile ^ step
            first, _ = first_tile_of(goal, spot[COLS + z])
            wanted = first + ((place - first) & 3)
            index = (lax.shift_right_arithmetic(tile, 2) ^ lax.shift_right_arithmetic(wanted, 2)) & 3
            out[z] = chosen(sources, index, z)


def pick(spot, *sources):
    return pl.pallas_call(
        pick_kernel,
        out_shape=[jax.ShapeDtypeStruct((2, 128, 128), BF)] * 4,
        in_specs=[pl.BlockSpec(memory_space=SMEM)] + [pl.BlockSpec(memory_space=VMEM)] * 4,
        out_specs=[pl.BlockSpec(memory_space=VMEM)] * 4,
        compiler_params=pltpu.CompilerParams(vmem_limit_bytes=8 * 1024 * 1024),
        cost_estimate=pl.CostEstimate(flops=0, bytes_accessed=16000000, transcendentals=0),
        name="pick",
    )(spot, *sources)


def align_kernel(spot, keep, one, two, three, both, to_chip, lifted):
    sources = (keep, one, two, three)
    tile = spot[TILE]
    lifted[0:32, :] = jnp.zeros((32, 256), F32)
    lifted[160:192, :] = jnp.zeros((32, 256), F32)
    lane = floor_lane((128, 128), 1)
    odd = spot[SEC] & 1
    for z in range(2):
        first, offset = first_tile_of(tile, spot[COLS + z])
        turned = []
        for k in range(3):
            inside = ((first + k >= 0) & (first + k < TILES)).astype(F32)
            value = chosen(sources, (tile ^ (first + k)) & 3, z).astype(F32) * inside
            turned.append(pltpu.roll(value, 128 - offset, 1))
        low = jnp.where(lane < 128 - offset, turned[0], turned[1])
        high = jnp.where(lane < 128 - offset, turned[1], turned[2])
        low = jnp.where((tile == 0) & (lane < HALO), 0.0, low)
        high = jnp.where((tile == TILES - 1) & (lane >= HALO), 0.0, high)
        lifted[32:160, 0:128] = low
        lifted[32:160, 128:256] = high
        base = pl.multiple_of(32 - BLK * spot[ROWS + z], BLK)
        window = lifted[pl.ds(base, 128), :].astype(BF)
        both[z] = window

        @pl.when(odd == z)
        def _():
            to_chip[0] = window


def align(spot, *sources):
    return pl.pallas_call(
        align_kernel,
        out_shape=[jax.ShapeDtypeStruct((n, 128, 256), BF) for n in (2, 1)],
        in_specs=[pl.BlockSpec(memory_space=SMEM)] + [pl.BlockSpec(memory_space=VMEM)] * 4,
        out_specs=[pl.BlockSpec(memory_space=VMEM)] * 2,
        scratch_shapes=[pltpu.VMEM((192, 256), F32)],
        compiler_params=pltpu.CompilerParams(vmem_limit_bytes=8 * 1024 * 1024),
        cost_estimate=pl.CostEstimate(flops=0, bytes_accessed=4000000, transcendentals=0),
        name="align",
    )(spot, *sources)


def front(tile, windows, w1, bias1, w2, bias2, ws, biass, left, right, feats, second, strided):
    count = len(windows)
    for side in (left, right):
        side[:, 0:2, :] = jnp.zeros((count, 2, 128), F32)
        side[:, 130:136, :] = jnp.zeros((count, 6, 128), F32)
    lane = floor_lane((32, 128), 1)
    patches = []
    for z in range(count):
        value = windows[z].astype(F32)
        left[z, 2:130, :] = value[:, 0:128]
        right[z, 2:130, :] = value[:, 128:256]
        made = [None] * SG
        for j in range(8):
            low = left[z, pl.ds(j, 32, stride=4), :]
            high = right[z, pl.ds(j, 32, stride=4), :]
            ring = jnp.where(lane < 8, high, low)
            mine = lane // 16 == j
            for g in range(SG):
                source = low if g < SG - 1 else ring
                shift = (16 * j - 12 * g) % 128
                turned = pltpu.roll(source, shift, 1) if shift else source
                made[g] = turned if j == 0 else jnp.where(mine, turned, made[g])
        patches += made
    patch = jnp.concatenate(patches, axis=0).astype(BF)
    groups = count * SG
    low_edge = tile == 0
    high_edge = tile == TILES - 1
    lane = floor_lane((32, 384), 1)
    for q in range(7):
        made = jnp.dot(patch, w1[:, 384 * q : 384 * (q + 1)], preferred_element_type=F32)
        made = jnp.maximum(made.reshape(groups, 32, 384) + bias1[...][None], 0.0)
        feats[:, 384 * q : 384 * (q + 1)] = made.reshape(groups * 32, 384).astype(BF)
        outside = {0: low_edge & (lane < 384), 1: low_edge & (lane < 192)}
        outside.update({5: high_edge & (lane >= 192), 6: high_edge & (lane >= 0)})
        if q in outside:
            for z in range(count):
                g = SG * z + (0 if q < 2 else SG - 1)
                kept = jnp.where(outside[q], 0.0, made[g])
                feats[32 * g : 32 * g + 32, 384 * q : 384 * (q + 1)] = kept.astype(BF)

    for p in range(6):
        made = jnp.dot(
            feats[:, 384 * p : 384 * p + 768], w2[...], preferred_element_type=F32
        )
        second[p] = jnp.maximum(made + bias2[...], 0.0).astype(BF)
    lane = floor_lane((1, 32, 128), 2)
    row = floor_lane((1, 32, 128), 1)
    from_above = (lane < 32) & (row > 0)
    from_below = (lane >= 96) & (row < 31)
    kept = (lane >= 32) & (lane < 96)
    for p in range(6):
        made = jnp.dot(second[p], ws[...], preferred_element_type=F32)
        made = jnp.maximum(made + biass[...], 0.0)
        down = pltpu.roll(made, 1, 0).reshape(groups, 32, 128)
        up = pltpu.roll(made, groups * 32 - 1, 0).reshape(groups, 32, 128)
        made = made.reshape(groups, 32, 128)
        made = jnp.where(kept, made, jnp.where(from_above, down, jnp.where(from_below, up, 0.0)))
        for g in range(groups):
            value = made[g]
            if p == 0 and g % SG == 0:
                value = jnp.where(low_edge, 0.0, value)
            if p == 5 and g % SG == SG - 1:
                value = jnp.where(high_edge, 0.0, value)
            strided[g // SG, p % 2, 3 * (g % SG) + p // 2] = value.astype(BF)


def own_kernel(
    spot, both, w1, bias1, w2, bias2, ws, biass, out, to_core, left, right, feats, second
):
    windows = (both[0], both[1])
    front(
        spot[TILE], windows, w1, bias1, w2, bias2, ws, biass, left, right, feats, second, out
    )
    odd = spot[SEC] & 1

    @pl.when(odd == 0)
    def _():
        to_core[0] = out[1]

    @pl.when(odd == 1)
    def _():
        to_core[0] = out[0]


def scratch(count):
    return [
        pltpu.VMEM((count, 136, 128), F32),
        pltpu.VMEM((count, 136, 128), F32),
        pltpu.VMEM((count * SG * 32, 2688), BF),
        pltpu.VMEM((6, count * SG * 32, 256), BF),
    ]


def features(count):
    return jax.ShapeDtypeStruct((count, 2, 33, 32, 128), BF)


def own(spot, both, *weights):
    return pl.pallas_call(
        own_kernel,
        out_shape=[features(2), features(1)],
        in_specs=[pl.BlockSpec(memory_space=SMEM)] + [pl.BlockSpec(memory_space=VMEM)] * 7,
        out_specs=[pl.BlockSpec(memory_space=VMEM)] * 2,
        scratch_shapes=scratch(2),
        compiler_params=pltpu.CompilerParams(vmem_limit_bytes=24 * 1024 * 1024),
        cost_estimate=pl.CostEstimate(flops=40000000000, bytes_accessed=4000000, transcendentals=0),
        name="own",
    )(spot, both, *weights)


def beyond_kernel(
    spot, window, w1, bias1, w2, bias2, ws, biass, out, left, right, feats, second
):
    sec = spot[SEC]
    front(
        spot[TILE], (window[0],), w1, bias1, w2, bias2, ws, biass, left, right, feats, second, out
    )

    @pl.when((sec == 0) | (sec == SECS - 1))
    def _():
        out[0] = jnp.zeros((2, 33, 32, 128), BF)


def beyond(spot, window, *weights):
    return pl.pallas_call(
        beyond_kernel,
        out_shape=features(1),
        in_specs=[pl.BlockSpec(memory_space=SMEM)] + [pl.BlockSpec(memory_space=VMEM)] * 7,
        out_specs=pl.BlockSpec(memory_space=VMEM),
        scratch_shapes=scratch(1),
        compiler_params=pltpu.CompilerParams(vmem_limit_bytes=24 * 1024 * 1024),
        cost_estimate=pl.CostEstimate(flops=20000000000, bytes_accessed=4000000, transcendentals=0),
        name="beyond",
    )(spot, window, *weights)


def main_kernel(spot, chip_side, core_side, middle, wd, biasd, wh, bh, out, outer, deeps):
    odd = spot[SEC] & 1
    outer[odd] = chip_side[0]
    outer[1 - odd] = core_side[0]
    for z in range(2):
        for part in range(4):
            blocks = []
            for dz in range(3):
                source = (outer.at[0], middle.at[0], middle.at[1], outer.at[1])[z + dz]
                for kx in range(4):
                    first = kx // 2 + 8 * part
                    blocks.append(source[kx % 2, first : first + 8].reshape(256, 128))
            patch = jnp.concatenate(blocks, axis=1)
            deep = jnp.dot(patch, wd[...], preferred_element_type=F32)
            deep = jnp.maximum(deep + biasd[...], 0.0)
            high = deep.astype(BF)
            deeps[z, part, :, 0:256] = high
            deeps[z, part, :, 256:512] = (deep - high.astype(F32)).astype(BF)
            deeps[z, part, :, 512:768] = high
    pair = lax.shift_right_logical(floor_lane((1, 8, 128), 2) & 63, 1)
    for z in range(2):
        spots = [jnp.zeros((4, 8, 128), F32)] * 3
        for part in range(4):
            logits = jnp.dot(deeps[z, part], wh[...], preferred_element_type=F32)
            for step in range(8):
                m = 8 * part + step
                slab = logits[32 * step : 32 * step + 32]
                for i in range(3):
                    shift = (2 * m - 2 * i) % 128
                    turned = pltpu.roll(slab, shift, 1) if shift else slab
                    spots[i] = jnp.where(pair == m, turned.reshape(4, 8, 128), spots[i])
        for i in range(3):
            value = spots[i].reshape(32, 128)
            for half in range(2):
                yp, k = divmod(2 * i + half, 3)
                if half == 1:
                    value = pltpu.roll(value, 64, 1)
                out[k, z, pl.ds(yp, 32, stride=2), :] = jax.nn.sigmoid(value[:, 0:64] + bh[k])


def main(spot, chip_side, core_side, middle, *weights):
    return pl.pallas_call(
        main_kernel,
        out_shape=jax.ShapeDtypeStruct((3, 2, 64, 64), F32),
        in_specs=[pl.BlockSpec(memory_space=SMEM)]
        + [pl.BlockSpec(memory_space=VMEM)] * 6
        + [pl.BlockSpec(memory_space=SMEM)],
        out_specs=pl.BlockSpec(memory_space=VMEM),
        scratch_shapes=[pltpu.VMEM((2, 2, 33, 32, 128), BF), pltpu.VMEM((2, 4, 256, 768), BF)],
        compiler_params=pltpu.CompilerParams(vmem_limit_bytes=24 * 1024 * 1024),
        name="convs",
    )(spot, chip_side, core_side, middle, *weights)


def prepare_kernel(*refs):
    small, t1, t2, ts = refs[:4]
    w1, bias1, w2, bias2, ws, biass = refs[4:]
    b1, b2, bs = (small[:, 32 * i : 32 * i + 32] for i in range(3))
    row = floor_lane((128, 384), 0)
    group = floor_lane((128, 384), 1) // 32
    dy = row // 16 - group % 6
    dx = row % 16 - group // 6
    base = jnp.zeros((128, 384), F32)
    for a in range(3):
        for b in range(3):
            spread = jnp.concatenate([t1[a, b : b + 1, :].astype(F32)] * 12, axis=1)
            base = jnp.where((dy == a) & (dx == b), spread, base)
    for q in range(7):
        turned = pltpu.roll(base, 2 * q, 0) if q else base
        w1[:, 384 * q : 384 * (q + 1)] = turned.astype(BF)
    lone = jnp.concatenate([b1] * 12, axis=1)
    row = floor_lane((32, 384), 0)
    group = floor_lane((32, 384), 1) // 32 % 6
    outside = ((row == 0) & (group == 0)) | ((row == 31) & (group == 5))
    bias1[...] = jnp.where(outside, OFF, lone)
    bias2[...] = jnp.concatenate([b2] * 8, axis=1)
    biass[...] = jnp.concatenate([bs] * 4, axis=1)

    lane = floor_lane((32, 128), 1)
    none = jnp.zeros((32, 128), F32)
    tiled = [
        [jnp.concatenate([t2[a, b].astype(F32).T] * 4, axis=1) for b in range(3)] for a in range(3)
    ]
    for kx in range(4):
        for xp in range(2):
            b = kx - xp
            for j in range(6):
                made = none
                if 0 <= b < 3:
                    for a in range(3):
                        if 0 <= j - a < 4:
                            made = jnp.where(lane // 32 == j - a, tiled[a][b], made)
                start = 32 * (6 * kx + j)
                w2[start : start + 32, 128 * xp : 128 * xp + 128] = made.astype(BF)

    tiled = [
        [jnp.concatenate([ts[a, b].astype(F32)] * 4, axis=1) for b in range(2)] for a in range(2)
    ]
    for xp in range(2):
        for yp in range(4):
            mine = (lane // 32) % 2 == (1 if yp < 2 else 0)
            start = 32 * (4 * xp + yp)
            ws[start : start + 32, :] = jnp.where(mine, tiled[yp % 2][xp], 0.0).astype(BF)


def prepare_deep_kernel(small, td, wd, biasd, wh):
    lane = floor_lane((32, 128), 1)
    none = jnp.zeros((32, 128), F32)
    biasd[...] = jnp.concatenate([small[3:4, :]] * 4, axis=1)
    for dz in range(3):
        tiled = [
            [jnp.concatenate([td[dz, a, b].astype(F32)] * 2, axis=1) for b in range(3)]
            for a in range(3)
        ]
        for kx in range(4):
            for xp in range(2):
                b = kx - xp
                for slot in range(4):
                    made = none
                    if 0 <= b < 3:
                        low = tiled[slot][b] if slot < 3 else none
                        high = tiled[slot - 1][b] if slot > 0 else none
                        made = jnp.where(lane < 64, low, high)
                    start = 128 * (4 * dz + kx) + 32 * slot
                    wd[start : start + 32, 128 * xp : 128 * xp + 128] = made.astype(BF)

    lane = floor_lane((64, 128), 1)
    heads = jnp.concatenate([small[0:3, :], jnp.zeros((5, 64), F32)], axis=0).T
    for xp in range(2):
        for yp in range(2):
            made = jnp.zeros((64, 128), F32)
            for k in range(3):
                c = 3 * yp + k
                made = jnp.where(lane == 64 * (c % 2) + 2 * (c // 2) + xp, heads[:, k : k + 1], made)
            high = made.astype(BF)
            low = (made - high.astype(F32)).astype(BF)
            start = 64 * (2 * xp + yp)
            wh[start : start + 64, :] = high
            wh[256 + start : 256 + start + 64, :] = high
            wh[512 + start : 512 + start + 64, :] = low


def prepare_deep(small, td):
    shape = jax.ShapeDtypeStruct
    return pl.pallas_call(
        prepare_deep_kernel,
        out_shape=(shape((1536, 256), BF), shape((1, 256), F32), shape((768, 128), BF)),
        in_specs=[pl.BlockSpec(memory_space=VMEM)] * 2,
        out_specs=[pl.BlockSpec(memory_space=VMEM)] * 3,
        compiler_params=pltpu.CompilerParams(vmem_limit_bytes=8 * 1024 * 1024),
        cost_estimate=pl.CostEstimate(flops=1000000, bytes_accessed=4000000, transcendentals=0),
        name="prepare_deep",
    )(small, td)


def prepare(small, w_first, w_second, ts):
    shape = jax.ShapeDtypeStruct
    return pl.pallas_call(
        prepare_kernel,
        out_shape=(
            shape((128, 2688), BF),
            shape((32, 384), F32),
            shape((768, 256), BF),
            shape((1, 256), F32),
            shape((256, 128), BF),
            shape((1, 128), F32),
        ),
        in_specs=[pl.BlockSpec(memory_space=VMEM)] * 4,
        out_specs=[pl.BlockSpec(memory_space=VMEM)] * 6,
        compiler_params=pltpu.CompilerParams(vmem_limit_bytes=16 * 1024 * 1024),
        cost_estimate=pl.CostEstimate(flops=1000000, bytes_accessed=4000000, transcendentals=0),
        name="prepare",
    )(
        small,
        jnp.transpose(w_first[:, 0], (1, 2, 0)),
        jnp.transpose(w_second, (2, 3, 0, 1)),
        ts,
    )


def local(
    raw_sections,
    shift_cols,
    shift_rows,
    w_first,
    b_first,
    w_second,
    b_second,
    w_stride,
    b_stride,
    w_depth,
    b_depth,
    w_head,
    b_head,
):
    place = jnp.stack([lax.axis_index("tile"), lax.axis_index("sec")])
    spot = jnp.concatenate([shift_cols, shift_rows, place.astype(jnp.int32)])
    small = jnp.concatenate([w_head, b_depth[None]], axis=0)
    deep = prepare_deep(small, jnp.transpose(w_depth, (2, 3, 4, 1, 0)))
    mine, ts, deep = lax.optimization_barrier(
        (stage(raw_sections), jnp.transpose(w_stride, (2, 3, 1, 0)), deep)
    )
    columns = [
        lax.ppermute(raw_sections, "tile", [(i, i ^ (4 * k)) for i in range(TILES)])
        for k in (1, 2, 3)
    ]
    keep, *sends = pick(spot, mine, *columns)
    sends, firsts, seconds = lax.optimization_barrier((sends, w_first, w_second))
    biases = jnp.concatenate([b_first, b_second, b_stride])[None]
    weights = prepare(biases, firsts, seconds, ts)
    pieces = [
        lax.ppermute(send, "tile", [(i, i ^ k) for i in range(TILES)])
        for k, send in zip((1, 2, 3), sends)
    ]
    both, to_chip = align(spot, keep, *pieces)
    window = lax.ppermute(
        to_chip, "sec", [(i, ((i + 1) ^ 1) - 1) for i in range(1, SECS - 1)]
    )
    middle, to_core = own(spot, both, *weights)
    core_side = lax.ppermute(to_core, "sec", [(i, i ^ 1) for i in range(SECS)])
    chip_side = beyond(spot, window, *weights)
    return main(spot, chip_side, core_side, middle, *deep, b_head)


def solution(mesh):
    in_specs = (P("sec", None, "tile"), P("sec"), P("sec")) + (P(),) * 10
    out_specs = P(None, "sec", None, "tile")
    return jax.shard_map(local, mesh=mesh, in_specs=in_specs, out_specs=out_specs, check_vma=False)
```

```python
import jax
import jax.numpy as jnp
from jax import lax
from jax.experimental import pallas as pl
from jax.experimental.pallas import tpu as pltpu
from jax.sharding import PartitionSpec as P

BLK = 16
TILES = 16
SECS = 16
HALO = 4
OFF = -1e30
BF = jnp.bfloat16
F32 = jnp.float32
SG = 11
VMEM = pltpu.VMEM
SMEM = pltpu.SMEM


COLS, ROWS, TILE, SEC = 0, 2, 4, 5


def floor_lane(shape, dim):
    return lax.broadcasted_iota(jnp.int32, shape, dim)


def first_tile_of(tile, shift):
    start = 128 * tile - BLK * shift - HALO
    first = lax.shift_right_arithmetic(start, 7)
    return first, start - first * 128


def chosen(sources, index, z):
    value = sources[0][z]
    for k in range(1, len(sources)):
        value = jnp.where(index == k, sources[k][z], value)
    return value


def stage_kernel(given, out):
    out[...] = given[...]


def stage(raw):
    return pl.pallas_call(
        stage_kernel,
        out_shape=jax.ShapeDtypeStruct(raw.shape, raw.dtype),
        in_specs=[pl.BlockSpec(memory_space=VMEM)],
        out_specs=pl.BlockSpec(memory_space=VMEM),
        compiler_params=pltpu.CompilerParams(vmem_limit_bytes=8 * 1024 * 1024),
        cost_estimate=pl.CostEstimate(flops=0, bytes_accessed=4000000, transcendentals=0),
        name="stage",
    )(raw)


def pick_kernel(spot, mine, one, two, three, keep, send_1, send_2, send_3):
    sources = (mine, one, two, three)
    tile = spot[TILE]
    place = tile & 3
    for z in range(2):
        for step, out in enumerate((keep, send_1, send_2, send_3)):
            goal = tile ^ step
            first, _ = first_tile_of(goal, spot[COLS + z])
            wanted = first + ((place - first) & 3)
            index = (lax.shift_right_arithmetic(tile, 2) ^ lax.shift_right_arithmetic(wanted, 2)) & 3
            out[z] = chosen(sources, index, z)


def pick(spot, *sources):
    return pl.pallas_call(
        pick_kernel,
        out_shape=[jax.ShapeDtypeStruct((2, 128, 128), BF)] * 4,
        in_specs=[pl.BlockSpec(memory_space=SMEM)] + [pl.BlockSpec(memory_space=VMEM)] * 4,
        out_specs=[pl.BlockSpec(memory_space=VMEM)] * 4,
        compiler_params=pltpu.CompilerParams(vmem_limit_bytes=8 * 1024 * 1024),
        cost_estimate=pl.CostEstimate(flops=0, bytes_accessed=16000000, transcendentals=0),
        name="pick",
    )(spot, *sources)


def align_kernel(
    spot, keep, one, two, three, w1, bias1, w2, bias2, ws, biass, both, to_chip, ahead,
    lifted, left, right, feats, second,
):
    sources = (keep, one, two, three)
    tile = spot[TILE]
    lifted[0:32, :] = jnp.zeros((32, 256), F32)
    lifted[160:192, :] = jnp.zeros((32, 256), F32)
    lane = floor_lane((128, 128), 1)
    odd = spot[SEC] & 1
    for z in range(2):
        first, offset = first_tile_of(tile, spot[COLS + z])
        turned = []
        for k in range(3):
            inside = ((first + k >= 0) & (first + k < TILES)).astype(F32)
            value = chosen(sources, (tile ^ (first + k)) & 3, z).astype(F32) * inside
            turned.append(pltpu.roll(value, 128 - offset, 1))
        low = jnp.where(lane < 128 - offset, turned[0], turned[1])
        high = jnp.where(lane < 128 - offset, turned[1], turned[2])
        low = jnp.where((tile == 0) & (lane < HALO), 0.0, low)
        high = jnp.where((tile == TILES - 1) & (lane >= HALO), 0.0, high)
        lifted[32:160, 0:128] = low
        lifted[32:160, 128:256] = high
        base = pl.multiple_of(32 - BLK * spot[ROWS + z], BLK)
        window = lifted[pl.ds(base, 128), :].astype(BF)
        both[z] = window

        @pl.when(odd == z)
        def _():
            to_chip[0] = window

    @pl.when(odd == 1)
    def _():
        front(
            tile, (both[0],), w1, bias1, w2, bias2, ws, biass, left, right, feats, second, ahead
        )


def align(spot, *sources):
    return pl.pallas_call(
        align_kernel,
        out_shape=[jax.ShapeDtypeStruct((n, 128, 256), BF) for n in (2, 1)] + [features(1)],
        in_specs=[pl.BlockSpec(memory_space=SMEM)] + [pl.BlockSpec(memory_space=VMEM)] * 10,
        out_specs=[pl.BlockSpec(memory_space=VMEM)] * 3,
        scratch_shapes=[pltpu.VMEM((192, 256), F32)] + scratch(1),
        compiler_params=pltpu.CompilerParams(vmem_limit_bytes=24 * 1024 * 1024),
        cost_estimate=pl.CostEstimate(flops=0, bytes_accessed=4000000, transcendentals=0),
        name="align",
    )(spot, *sources)


def front(tile, windows, w1, bias1, w2, bias2, ws, biass, left, right, feats, second, strided):
    count = len(windows)
    for side in (left, right):
        side[:, 0:2, :] = jnp.zeros((count, 2, 128), F32)
        side[:, 130:136, :] = jnp.zeros((count, 6, 128), F32)
    lane = floor_lane((32, 128), 1)
    patches = []
    for z in range(count):
        value = windows[z].astype(F32)
        left[z, 2:130, :] = value[:, 0:128]
        right[z, 2:130, :] = value[:, 128:256]
        made = [None] * SG
        for j in range(8):
            low = left[z, pl.ds(j, 32, stride=4), :]
            high = right[z, pl.ds(j, 32, stride=4), :]
            ring = jnp.where(lane < 8, high, low)
            mine = lane // 16 == j
            for g in range(SG):
                source = low if g < SG - 1 else ring
                shift = (16 * j - 12 * g) % 128
                turned = pltpu.roll(source, shift, 1) if shift else source
                made[g] = turned if j == 0 else jnp.where(mine, turned, made[g])
        patches += made
    patch = jnp.concatenate(patches, axis=0).astype(BF)
    groups = count * SG
    low_edge = tile == 0
    high_edge = tile == TILES - 1
    lane = floor_lane((32, 384), 1)
    for q in range(7):
        made = jnp.dot(patch, w1[:, 384 * q : 384 * (q + 1)], preferred_element_type=F32)
        made = jnp.maximum(made.reshape(groups, 32, 384) + bias1[...][None], 0.0)
        feats[:, 384 * q : 384 * (q + 1)] = made.reshape(groups * 32, 384).astype(BF)
        outside = {0: low_edge & (lane < 384), 1: low_edge & (lane < 192)}
        outside.update({5: high_edge & (lane >= 192), 6: high_edge & (lane >= 0)})
        if q in outside:
            for z in range(count):
                g = SG * z + (0 if q < 2 else SG - 1)
                kept = jnp.where(outside[q], 0.0, made[g])
                feats[32 * g : 32 * g + 32, 384 * q : 384 * (q + 1)] = kept.astype(BF)

    for p in range(6):
        made = jnp.dot(
            feats[:, 384 * p : 384 * p + 768], w2[...], preferred_element_type=F32
        )
        second[p] = jnp.maximum(made + bias2[...], 0.0).astype(BF)
    lane = floor_lane((1, 32, 128), 2)
    row = floor_lane((1, 32, 128), 1)
    from_above = (lane < 32) & (row > 0)
    from_below = (lane >= 96) & (row < 31)
    kept = (lane >= 32) & (lane < 96)
    for p in range(6):
        made = jnp.dot(second[p], ws[...], preferred_element_type=F32)
        made = jnp.maximum(made + biass[...], 0.0)
        down = pltpu.roll(made, 1, 0).reshape(groups, 32, 128)
        up = pltpu.roll(made, groups * 32 - 1, 0).reshape(groups, 32, 128)
        made = made.reshape(groups, 32, 128)
        made = jnp.where(kept, made, jnp.where(from_above, down, jnp.where(from_below, up, 0.0)))
        for g in range(groups):
            value = made[g]
            if p == 0 and g % SG == 0:
                value = jnp.where(low_edge, 0.0, value)
            if p == 5 and g % SG == SG - 1:
                value = jnp.where(high_edge, 0.0, value)
            strided[g // SG, p % 2, 3 * (g % SG) + p // 2] = value.astype(BF)


def own_kernel(
    spot, both, ahead, w1, bias1, w2, bias2, ws, biass, out, to_core, left, right, feats, second
):
    tile = spot[TILE]
    odd = spot[SEC] & 1

    @pl.when(odd == 0)
    def _():
        windows = (both[0], both[1])
        front(tile, windows, w1, bias1, w2, bias2, ws, biass, left, right, feats, second, out)
        to_core[0] = out[1]

    @pl.when(odd == 1)
    def _():
        front(
            tile, (both[1],), w1, bias1, w2, bias2, ws, biass,
            left.at[0:1], right.at[0:1], feats.at[0 : SG * 32], second.at[:, 0 : SG * 32], out.at[1:2],
        )
        out[0] = ahead[0]
        to_core[0] = ahead[0]


def scratch(count):
    return [
        pltpu.VMEM((count, 136, 128), F32),
        pltpu.VMEM((count, 136, 128), F32),
        pltpu.VMEM((count * SG * 32, 2688), BF),
        pltpu.VMEM((6, count * SG * 32, 256), BF),
    ]


def features(count):
    return jax.ShapeDtypeStruct((count, 2, 33, 32, 128), BF)


def own(spot, both, ahead, *weights):
    return pl.pallas_call(
        own_kernel,
        out_shape=[features(2), features(1)],
        in_specs=[pl.BlockSpec(memory_space=SMEM)] + [pl.BlockSpec(memory_space=VMEM)] * 8,
        out_specs=[pl.BlockSpec(memory_space=VMEM)] * 2,
        scratch_shapes=scratch(2),
        compiler_params=pltpu.CompilerParams(vmem_limit_bytes=24 * 1024 * 1024),
        cost_estimate=pl.CostEstimate(flops=40000000000, bytes_accessed=4000000, transcendentals=0),
        name="own",
    )(spot, both, ahead, *weights)


def beyond_kernel(
    spot, window, w1, bias1, w2, bias2, ws, biass, out, left, right, feats, second
):
    sec = spot[SEC]
    front(
        spot[TILE], (window[0],), w1, bias1, w2, bias2, ws, biass, left, right, feats, second, out
    )

    @pl.when((sec == 0) | (sec == SECS - 1))
    def _():
        out[0] = jnp.zeros((2, 33, 32, 128), BF)


def beyond(spot, window, *weights):
    return pl.pallas_call(
        beyond_kernel,
        out_shape=features(1),
        in_specs=[pl.BlockSpec(memory_space=SMEM)] + [pl.BlockSpec(memory_space=VMEM)] * 7,
        out_specs=pl.BlockSpec(memory_space=VMEM),
        scratch_shapes=scratch(1),
        compiler_params=pltpu.CompilerParams(vmem_limit_bytes=24 * 1024 * 1024),
        cost_estimate=pl.CostEstimate(flops=20000000000, bytes_accessed=4000000, transcendentals=0),
        name="beyond",
    )(spot, window, *weights)


def main_kernel(spot, chip_side, core_side, middle, wd, biasd, wh, bh, out, outer, deeps):
    odd = spot[SEC] & 1
    outer[odd] = chip_side[0]
    outer[1 - odd] = core_side[0]
    for z in range(2):
        for part in range(4):
            blocks = []
            for dz in range(3):
                source = (outer.at[0], middle.at[0], middle.at[1], outer.at[1])[z + dz]
                for kx in range(4):
                    first = kx // 2 + 8 * part
                    blocks.append(source[kx % 2, first : first + 8].reshape(256, 128))
            patch = jnp.concatenate(blocks, axis=1)
            deep = jnp.dot(patch, wd[...], preferred_element_type=F32)
            deep = jnp.maximum(deep + biasd[...], 0.0)
            high = deep.astype(BF)
            deeps[z, part, :, 0:256] = high
            deeps[z, part, :, 256:512] = (deep - high.astype(F32)).astype(BF)
            deeps[z, part, :, 512:768] = high
    pair = lax.shift_right_logical(floor_lane((1, 8, 128), 2) & 63, 1)
    for z in range(2):
        spots = [jnp.zeros((4, 8, 128), F32)] * 3
        for part in range(4):
            logits = jnp.dot(deeps[z, part], wh[...], preferred_element_type=F32)
            for step in range(8):
                m = 8 * part + step
                slab = logits[32 * step : 32 * step + 32]
                for i in range(3):
                    shift = (2 * m - 2 * i) % 128
                    turned = pltpu.roll(slab, shift, 1) if shift else slab
                    spots[i] = jnp.where(pair == m, turned.reshape(4, 8, 128), spots[i])
        for i in range(3):
            value = spots[i].reshape(32, 128)
            for half in range(2):
                yp, k = divmod(2 * i + half, 3)
                if half == 1:
                    value = pltpu.roll(value, 64, 1)
                out[k, z, pl.ds(yp, 32, stride=2), :] = jax.nn.sigmoid(value[:, 0:64] + bh[k])


def main(spot, chip_side, core_side, middle, *weights):
    return pl.pallas_call(
        main_kernel,
        out_shape=jax.ShapeDtypeStruct((3, 2, 64, 64), F32),
        in_specs=[pl.BlockSpec(memory_space=SMEM)]
        + [pl.BlockSpec(memory_space=VMEM)] * 6
        + [pl.BlockSpec(memory_space=SMEM)],
        out_specs=pl.BlockSpec(memory_space=VMEM),
        scratch_shapes=[pltpu.VMEM((2, 2, 33, 32, 128), BF), pltpu.VMEM((2, 4, 256, 768), BF)],
        compiler_params=pltpu.CompilerParams(vmem_limit_bytes=24 * 1024 * 1024),
        name="convs",
    )(spot, chip_side, core_side, middle, *weights)


def prepare_kernel(*refs):
    small, t1, t2, ts = refs[:4]
    w1, bias1, w2, bias2, ws, biass = refs[4:]
    b1, b2, bs = (small[:, 32 * i : 32 * i + 32] for i in range(3))
    row = floor_lane((128, 384), 0)
    group = floor_lane((128, 384), 1) // 32
    dy = row // 16 - group % 6
    dx = row % 16 - group // 6
    base = jnp.zeros((128, 384), F32)
    for a in range(3):
        for b in range(3):
            spread = jnp.concatenate([t1[a, b : b + 1, :].astype(F32)] * 12, axis=1)
            base = jnp.where((dy == a) & (dx == b), spread, base)
    for q in range(7):
        turned = pltpu.roll(base, 2 * q, 0) if q else base
        w1[:, 384 * q : 384 * (q + 1)] = turned.astype(BF)
    lone = jnp.concatenate([b1] * 12, axis=1)
    row = floor_lane((32, 384), 0)
    group = floor_lane((32, 384), 1) // 32 % 6
    outside = ((row == 0) & (group == 0)) | ((row == 31) & (group == 5))
    bias1[...] = jnp.where(outside, OFF, lone)
    bias2[...] = jnp.concatenate([b2] * 8, axis=1)
    biass[...] = jnp.concatenate([bs] * 4, axis=1)

    lane = floor_lane((32, 128), 1)
    none = jnp.zeros((32, 128), F32)
    tiled = [
        [jnp.concatenate([t2[a, b].astype(F32).T] * 4, axis=1) for b in range(3)] for a in range(3)
    ]
    for kx in range(4):
        for xp in range(2):
            b = kx - xp
            for j in range(6):
                made = none
                if 0 <= b < 3:
                    for a in range(3):
                        if 0 <= j - a < 4:
                            made = jnp.where(lane // 32 == j - a, tiled[a][b], made)
                start = 32 * (6 * kx + j)
                w2[start : start + 32, 128 * xp : 128 * xp + 128] = made.astype(BF)

    tiled = [
        [jnp.concatenate([ts[a, b].astype(F32)] * 4, axis=1) for b in range(2)] for a in range(2)
    ]
    for xp in range(2):
        for yp in range(4):
            mine = (lane // 32) % 2 == (1 if yp < 2 else 0)
            start = 32 * (4 * xp + yp)
            ws[start : start + 32, :] = jnp.where(mine, tiled[yp % 2][xp], 0.0).astype(BF)


def prepare_deep_kernel(small, td, wd, biasd, wh):
    lane = floor_lane((32, 128), 1)
    none = jnp.zeros((32, 128), F32)
    biasd[...] = jnp.concatenate([small[3:4, :]] * 4, axis=1)
    for dz in range(3):
        tiled = [
            [jnp.concatenate([td[dz, a, b].astype(F32)] * 2, axis=1) for b in range(3)]
            for a in range(3)
        ]
        for kx in range(4):
            for xp in range(2):
                b = kx - xp
                for slot in range(4):
                    made = none
                    if 0 <= b < 3:
                        low = tiled[slot][b] if slot < 3 else none
                        high = tiled[slot - 1][b] if slot > 0 else none
                        made = jnp.where(lane < 64, low, high)
                    start = 128 * (4 * dz + kx) + 32 * slot
                    wd[start : start + 32, 128 * xp : 128 * xp + 128] = made.astype(BF)

    lane = floor_lane((64, 128), 1)
    heads = jnp.concatenate([small[0:3, :], jnp.zeros((5, 64), F32)], axis=0).T
    for xp in range(2):
        for yp in range(2):
            made = jnp.zeros((64, 128), F32)
            for k in range(3):
                c = 3 * yp + k
                made = jnp.where(lane == 64 * (c % 2) + 2 * (c // 2) + xp, heads[:, k : k + 1], made)
            high = made.astype(BF)
            low = (made - high.astype(F32)).astype(BF)
            start = 64 * (2 * xp + yp)
            wh[start : start + 64, :] = high
            wh[256 + start : 256 + start + 64, :] = high
            wh[512 + start : 512 + start + 64, :] = low


def prepare_deep(small, td):
    shape = jax.ShapeDtypeStruct
    return pl.pallas_call(
        prepare_deep_kernel,
        out_shape=(shape((1536, 256), BF), shape((1, 256), F32), shape((768, 128), BF)),
        in_specs=[pl.BlockSpec(memory_space=VMEM)] * 2,
        out_specs=[pl.BlockSpec(memory_space=VMEM)] * 3,
        compiler_params=pltpu.CompilerParams(vmem_limit_bytes=8 * 1024 * 1024),
        cost_estimate=pl.CostEstimate(flops=1000000, bytes_accessed=4000000, transcendentals=0),
        name="prepare_deep",
    )(small, td)


def prepare(small, w_first, w_second, ts):
    shape = jax.ShapeDtypeStruct
    return pl.pallas_call(
        prepare_kernel,
        out_shape=(
            shape((128, 2688), BF),
            shape((32, 384), F32),
            shape((768, 256), BF),
            shape((1, 256), F32),
            shape((256, 128), BF),
            shape((1, 128), F32),
        ),
        in_specs=[pl.BlockSpec(memory_space=VMEM)] * 4,
        out_specs=[pl.BlockSpec(memory_space=VMEM)] * 6,
        compiler_params=pltpu.CompilerParams(vmem_limit_bytes=16 * 1024 * 1024),
        cost_estimate=pl.CostEstimate(flops=1000000, bytes_accessed=4000000, transcendentals=0),
        name="prepare",
    )(
        small,
        jnp.transpose(w_first[:, 0], (1, 2, 0)),
        jnp.transpose(w_second, (2, 3, 0, 1)),
        ts,
    )


def local(
    raw_sections,
    shift_cols,
    shift_rows,
    w_first,
    b_first,
    w_second,
    b_second,
    w_stride,
    b_stride,
    w_depth,
    b_depth,
    w_head,
    b_head,
):
    place = jnp.stack([lax.axis_index("tile"), lax.axis_index("sec")])
    spot = jnp.concatenate([shift_cols, shift_rows, place.astype(jnp.int32)])
    small = jnp.concatenate([w_head, b_depth[None]], axis=0)
    deep = prepare_deep(small, jnp.transpose(w_depth, (2, 3, 4, 1, 0)))
    mine, ts, deep = lax.optimization_barrier(
        (stage(raw_sections), jnp.transpose(w_stride, (2, 3, 1, 0)), deep)
    )
    columns = [
        lax.ppermute(raw_sections, "tile", [(i, i ^ (4 * k)) for i in range(TILES)])
        for k in (1, 2, 3)
    ]
    keep, *sends = pick(spot, mine, *columns)
    sends, firsts, seconds = lax.optimization_barrier((sends, w_first, w_second))
    biases = jnp.concatenate([b_first, b_second, b_stride])[None]
    weights = prepare(biases, firsts, seconds, ts)
    pieces = [
        lax.ppermute(send, "tile", [(i, i ^ k) for i in range(TILES)])
        for k, send in zip((1, 2, 3), sends)
    ]
    both, to_chip, ahead = align(spot, keep, *pieces, *weights)
    window = lax.ppermute(
        to_chip, "sec", [(i, ((i + 1) ^ 1) - 1) for i in range(1, SECS - 1)]
    )
    middle, to_core = own(spot, both, ahead, *weights)
    core_side = lax.ppermute(to_core, "sec", [(i, i ^ 1) for i in range(SECS)])
    chip_side = beyond(spot, window, *weights)
    return main(spot, chip_side, core_side, middle, *deep, b_head)


def solution(mesh):
    in_specs = (P("sec", None, "tile"), P("sec"), P("sec")) + (P(),) * 10
    out_specs = P(None, "sec", None, "tile")
    return jax.shard_map(local, mesh=mesh, in_specs=in_specs, out_specs=out_specs, check_vma=False)
```

```python
import jax
import jax.numpy as jnp
from jax import lax
from jax.experimental import pallas as pl
from jax.experimental.pallas import tpu as pltpu
from jax.sharding import PartitionSpec as P

BLK = 16
TILES = 16
SECS = 16
HALO = 4
OFF = -1e30
BF = jnp.bfloat16
F32 = jnp.float32
SG = 11
VMEM = pltpu.VMEM
SMEM = pltpu.SMEM


COLS, ROWS, TILE, SEC = 0, 2, 4, 5


def floor_lane(shape, dim):
    return lax.broadcasted_iota(jnp.int32, shape, dim)


def first_tile_of(tile, shift):
    start = 128 * tile - BLK * shift - HALO
    first = lax.shift_right_arithmetic(start, 7)
    return first, start - first * 128


def chosen(sources, index, z):
    value = sources[0][z]
    for k in range(1, len(sources)):
        value = jnp.where(index == k, sources[k][z], value)
    return value


def stage_kernel(given, out):
    out[...] = given[...]


def stage(raw):
    return pl.pallas_call(
        stage_kernel,
        out_shape=jax.ShapeDtypeStruct(raw.shape, raw.dtype),
        in_specs=[pl.BlockSpec(memory_space=VMEM)],
        out_specs=pl.BlockSpec(memory_space=VMEM),
        compiler_params=pltpu.CompilerParams(vmem_limit_bytes=8 * 1024 * 1024),
        cost_estimate=pl.CostEstimate(flops=0, bytes_accessed=4000000, transcendentals=0),
        name="stage",
    )(raw)


def pick_kernel(spot, mine, one, two, three, keep, send_1, send_2, send_3):
    sources = (mine, one, two, three)
    tile = spot[TILE]
    place = tile & 3
    for z in range(2):
        for step, out in enumerate((keep, send_1, send_2, send_3)):
            goal = tile ^ step
            first, _ = first_tile_of(goal, spot[COLS + z])
            wanted = first + ((place - first) & 3)
            index = (lax.shift_right_arithmetic(tile, 2) ^ lax.shift_right_arithmetic(wanted, 2)) & 3
            out[z] = chosen(sources, index, z)


def pick(spot, *sources):
    return pl.pallas_call(
        pick_kernel,
        out_shape=[jax.ShapeDtypeStruct((2, 128, 128), BF)] * 4,
        in_specs=[pl.BlockSpec(memory_space=SMEM)] + [pl.BlockSpec(memory_space=VMEM)] * 4,
        out_specs=[pl.BlockSpec(memory_space=VMEM)] * 4,
        compiler_params=pltpu.CompilerParams(vmem_limit_bytes=8 * 1024 * 1024),
        cost_estimate=pl.CostEstimate(flops=0, bytes_accessed=16000000, transcendentals=0),
        name="pick",
    )(spot, *sources)


def align_kernel(
    spot, keep, one, two, three, w1, bias1, w2, bias2, ws, biass, both, to_chip, ahead,
    lifted, left, right, feats, second,
):
    sources = (keep, one, two, three)
    tile = spot[TILE]
    lifted[0:32, :] = jnp.zeros((32, 256), F32)
    lifted[160:192, :] = jnp.zeros((32, 256), F32)
    lane = floor_lane((128, 128), 1)
    odd = spot[SEC] & 1
    for z in range(2):
        first, offset = first_tile_of(tile, spot[COLS + z])
        turned = []
        for k in range(3):
            inside = ((first + k >= 0) & (first + k < TILES)).astype(F32)
            value = chosen(sources, (tile ^ (first + k)) & 3, z).astype(F32) * inside
            turned.append(pltpu.roll(value, 128 - offset, 1))
        low = jnp.where(lane < 128 - offset, turned[0], turned[1])
        high = jnp.where(lane < 128 - offset, turned[1], turned[2])
        low = jnp.where((tile == 0) & (lane < HALO), 0.0, low)
        high = jnp.where((tile == TILES - 1) & (lane >= HALO), 0.0, high)
        lifted[32:160, 0:128] = low
        lifted[32:160, 128:256] = high
        base = pl.multiple_of(32 - BLK * spot[ROWS + z], BLK)
        window = lifted[pl.ds(base, 128), :].astype(BF)
        both[z] = window

        @pl.when(odd == z)
        def _():
            to_chip[0] = window

    @pl.when(odd == 1)
    def _():
        front(
            tile, (both[0],), w1, bias1, w2, bias2, ws, biass, left, right, feats, second, ahead
        )


def align(spot, *sources):
    return pl.pallas_call(
        align_kernel,
        out_shape=[jax.ShapeDtypeStruct((n, 128, 256), BF) for n in (2, 1)] + [features(1)],
        in_specs=[pl.BlockSpec(memory_space=SMEM)] + [pl.BlockSpec(memory_space=VMEM)] * 10,
        out_specs=[pl.BlockSpec(memory_space=VMEM)] * 3,
        scratch_shapes=[pltpu.VMEM((192, 256), F32)] + scratch(1),
        compiler_params=pltpu.CompilerParams(vmem_limit_bytes=24 * 1024 * 1024),
        cost_estimate=pl.CostEstimate(flops=0, bytes_accessed=4000000, transcendentals=0),
        name="align",
    )(spot, *sources)


def front(tile, windows, w1, bias1, w2, bias2, ws, biass, left, right, feats, second, strided):
    count = len(windows)
    for side in (left, right):
        side[:, 0:2, :] = jnp.zeros((count, 2, 128), F32)
        side[:, 130:136, :] = jnp.zeros((count, 6, 128), F32)
    lane = floor_lane((32, 128), 1)
    patches = []
    for z in range(count):
        value = windows[z].astype(F32)
        left[z, 2:130, :] = value[:, 0:128]
        right[z, 2:130, :] = value[:, 128:256]
        made = [None] * SG
        for j in range(8):
            low = left[z, pl.ds(j, 32, stride=4), :]
            high = right[z, pl.ds(j, 32, stride=4), :]
            ring = jnp.where(lane < 8, high, low)
            mine = lane // 16 == j
            for g in range(SG):
                source = low if g < SG - 1 else ring
                shift = (16 * j - 12 * g) % 128
                turned = pltpu.roll(source, shift, 1) if shift else source
                made[g] = turned if j == 0 else jnp.where(mine, turned, made[g])
        patches += made
    patch = jnp.concatenate(patches, axis=0).astype(BF)
    groups = count * SG
    low_edge = tile == 0
    high_edge = tile == TILES - 1
    lane = floor_lane((32, 384), 1)
    for q in range(7):
        made = jnp.dot(patch, w1[:, 384 * q : 384 * (q + 1)], preferred_element_type=F32)
        made = jnp.maximum(made.reshape(groups, 32, 384) + bias1[...][None], 0.0)
        feats[:, 384 * q : 384 * (q + 1)] = made.reshape(groups * 32, 384).astype(BF)
        outside = {0: low_edge & (lane < 384), 1: low_edge & (lane < 192)}
        outside.update({5: high_edge & (lane >= 192), 6: high_edge & (lane >= 0)})
        if q in outside:
            for z in range(count):
                g = SG * z + (0 if q < 2 else SG - 1)
                kept = jnp.where(outside[q], 0.0, made[g])
                feats[32 * g : 32 * g + 32, 384 * q : 384 * (q + 1)] = kept.astype(BF)

    for p in range(6):
        made = jnp.dot(
            feats[:, 384 * p : 384 * p + 768], w2[...], preferred_element_type=F32
        )
        second[p] = jnp.maximum(made + bias2[...], 0.0).astype(BF)
    lane = floor_lane((1, 32, 128), 2)
    row = floor_lane((1, 32, 128), 1)
    from_above = (lane < 32) & (row > 0)
    from_below = (lane >= 96) & (row < 31)
    kept = (lane >= 32) & (lane < 96)
    for p in range(6):
        made = jnp.dot(second[p], ws[...], preferred_element_type=F32)
        made = jnp.maximum(made + biass[...], 0.0)
        down = pltpu.roll(made, 1, 0).reshape(groups, 32, 128)
        up = pltpu.roll(made, groups * 32 - 1, 0).reshape(groups, 32, 128)
        made = made.reshape(groups, 32, 128)
        made = jnp.where(kept, made, jnp.where(from_above, down, jnp.where(from_below, up, 0.0)))
        for g in range(groups):
            value = made[g]
            if p == 0 and g % SG == 0:
                value = jnp.where(low_edge, 0.0, value)
            if p == 5 and g % SG == SG - 1:
                value = jnp.where(high_edge, 0.0, value)
            strided[g // SG, p % 2, 3 * (g % SG) + p // 2] = value.astype(BF)


def own_kernel(
    spot, both, ahead, w1, bias1, w2, bias2, ws, biass, out, to_core, left, right, feats, second
):
    tile = spot[TILE]
    odd = spot[SEC] & 1

    @pl.when(odd == 0)
    def _():
        windows = (both[0], both[1])
        front(tile, windows, w1, bias1, w2, bias2, ws, biass, left, right, feats, second, out)
        to_core[0] = out[1]

    @pl.when(odd == 1)
    def _():
        front(
            tile, (both[1],), w1, bias1, w2, bias2, ws, biass,
            left.at[0:1], right.at[0:1], feats.at[0 : SG * 32], second.at[:, 0 : SG * 32], out.at[1:2],
        )
        out[0] = ahead[0]
        to_core[0] = ahead[0]


def scratch(count):
    return [
        pltpu.VMEM((count, 136, 128), F32),
        pltpu.VMEM((count, 136, 128), F32),
        pltpu.VMEM((count * SG * 32, 2688), BF),
        pltpu.VMEM((6, count * SG * 32, 256), BF),
    ]


def features(count):
    return jax.ShapeDtypeStruct((count, 2, 33, 32, 128), BF)


def own(spot, both, ahead, *weights):
    return pl.pallas_call(
        own_kernel,
        out_shape=[features(2), features(1)],
        in_specs=[pl.BlockSpec(memory_space=SMEM)] + [pl.BlockSpec(memory_space=VMEM)] * 8,
        out_specs=[pl.BlockSpec(memory_space=VMEM)] * 2,
        scratch_shapes=scratch(2),
        compiler_params=pltpu.CompilerParams(vmem_limit_bytes=24 * 1024 * 1024),
        cost_estimate=pl.CostEstimate(flops=40000000000, bytes_accessed=4000000, transcendentals=0),
        name="own",
    )(spot, both, ahead, *weights)


def beyond_kernel(
    spot, window, w1, bias1, w2, bias2, ws, biass, out, left, right, feats, second
):
    sec = spot[SEC]
    front(
        spot[TILE], (window[0],), w1, bias1, w2, bias2, ws, biass, left, right, feats, second, out
    )

    @pl.when((sec == 0) | (sec == SECS - 1))
    def _():
        out[0] = jnp.zeros((2, 33, 32, 128), BF)


def beyond(spot, window, *weights):
    return pl.pallas_call(
        beyond_kernel,
        out_shape=features(1),
        in_specs=[pl.BlockSpec(memory_space=SMEM)] + [pl.BlockSpec(memory_space=VMEM)] * 7,
        out_specs=pl.BlockSpec(memory_space=VMEM),
        scratch_shapes=scratch(1),
        compiler_params=pltpu.CompilerParams(vmem_limit_bytes=24 * 1024 * 1024),
        cost_estimate=pl.CostEstimate(flops=20000000000, bytes_accessed=4000000, transcendentals=0),
        name="beyond",
    )(spot, window, *weights)


def main_kernel(spot, chip_side, core_side, middle, wd, biasd, wh, bh, out, outer, deeps):
    odd = spot[SEC] & 1
    outer[odd] = chip_side[0]
    outer[1 - odd] = core_side[0]
    for z in range(2):
        for part in range(4):
            blocks = []
            for dz in range(3):
                source = (outer.at[0], middle.at[0], middle.at[1], outer.at[1])[z + dz]
                for kx in range(4):
                    first = kx // 2 + 8 * part
                    blocks.append(source[kx % 2, first : first + 8].reshape(256, 128))
            patch = jnp.concatenate(blocks, axis=1)
            deep = jnp.dot(patch, wd[...], preferred_element_type=F32)
            deep = jnp.maximum(deep + biasd[...], 0.0)
            high = deep.astype(BF)
            low = (deep - high.astype(F32)).astype(BF)
            for m in range(8):
                here = slice(32 * m, 32 * m + 32)
                rows = pl.ds(32 * (8 * z + 2 * part + m // 4), 32)
                at = 512 * (m % 4)
                deeps[rows, at : at + 256] = high[here]
                deeps[rows, at + 256 : at + 512] = low[here]
    block = lax.shift_right_logical(floor_lane((1, 8, 128), 2) & 63, 3)
    for z in range(2):
        logits = jnp.dot(deeps[256 * z : 256 * z + 256], wh[...], preferred_element_type=F32)
        logits = logits + pltpu.roll(logits, 96, 1)
        spots = [jnp.zeros((4, 8, 128), F32)] * 3
        for part in range(8):
            slab = logits[32 * part : 32 * part + 32]
            for i in range(3):
                shift = 8 * (part - i) % 128
                turned = pltpu.roll(slab, shift, 1) if shift else slab
                spots[i] = jnp.where(block == part, turned.reshape(4, 8, 128), spots[i])
        for i in range(3):
            value = spots[i].reshape(32, 128)
            for half in range(2):
                yp, k = divmod(2 * i + half, 3)
                if half == 1:
                    value = pltpu.roll(value, 64, 1)
                out[k, z, pl.ds(yp, 32, stride=2), :] = jax.nn.sigmoid(value[:, 0:64] + bh[k])


def main(spot, chip_side, core_side, middle, *weights):
    return pl.pallas_call(
        main_kernel,
        out_shape=jax.ShapeDtypeStruct((3, 2, 64, 64), F32),
        in_specs=[pl.BlockSpec(memory_space=SMEM)]
        + [pl.BlockSpec(memory_space=VMEM)] * 6
        + [pl.BlockSpec(memory_space=SMEM)],
        out_specs=pl.BlockSpec(memory_space=VMEM),
        scratch_shapes=[pltpu.VMEM((2, 2, 33, 32, 128), BF), pltpu.VMEM((512, 2048), BF)],
        compiler_params=pltpu.CompilerParams(vmem_limit_bytes=24 * 1024 * 1024),
        name="convs",
    )(spot, chip_side, core_side, middle, *weights)


def prepare_kernel(*refs):
    small, t1, t2, ts = refs[:4]
    w1, bias1, w2, bias2, ws, biass = refs[4:]
    b1, b2, bs = (small[:, 32 * i : 32 * i + 32] for i in range(3))
    row = floor_lane((128, 384), 0)
    group = floor_lane((128, 384), 1) // 32
    dy = row // 16 - group % 6
    dx = row % 16 - group // 6
    base = jnp.zeros((128, 384), F32)
    for a in range(3):
        for b in range(3):
            spread = jnp.concatenate([t1[a, b : b + 1, :].astype(F32)] * 12, axis=1)
            base = jnp.where((dy == a) & (dx == b), spread, base)
    for q in range(7):
        turned = pltpu.roll(base, 2 * q, 0) if q else base
        w1[:, 384 * q : 384 * (q + 1)] = turned.astype(BF)
    lone = jnp.concatenate([b1] * 12, axis=1)
    row = floor_lane((32, 384), 0)
    group = floor_lane((32, 384), 1) // 32 % 6
    outside = ((row == 0) & (group == 0)) | ((row == 31) & (group == 5))
    bias1[...] = jnp.where(outside, OFF, lone)
    bias2[...] = jnp.concatenate([b2] * 8, axis=1)
    biass[...] = jnp.concatenate([bs] * 4, axis=1)

    lane = floor_lane((32, 128), 1)
    none = jnp.zeros((32, 128), F32)
    tiled = [
        [jnp.concatenate([t2[a, b].astype(F32).T] * 4, axis=1) for b in range(3)] for a in range(3)
    ]
    for kx in range(4):
        for xp in range(2):
            b = kx - xp
            for j in range(6):
                made = none
                if 0 <= b < 3:
                    for a in range(3):
                        if 0 <= j - a < 4:
                            made = jnp.where(lane // 32 == j - a, tiled[a][b], made)
                start = 32 * (6 * kx + j)
                w2[start : start + 32, 128 * xp : 128 * xp + 128] = made.astype(BF)

    tiled = [
        [jnp.concatenate([ts[a, b].astype(F32)] * 4, axis=1) for b in range(2)] for a in range(2)
    ]
    for xp in range(2):
        for yp in range(4):
            mine = (lane // 32) % 2 == (1 if yp < 2 else 0)
            start = 32 * (4 * xp + yp)
            ws[start : start + 32, :] = jnp.where(mine, tiled[yp % 2][xp], 0.0).astype(BF)


def prepare_deep_kernel(small, td, wd, biasd, wh):
    lane = floor_lane((32, 128), 1)
    none = jnp.zeros((32, 128), F32)
    biasd[...] = jnp.concatenate([small[3:4, :]] * 4, axis=1)
    for dz in range(3):
        tiled = [
            [jnp.concatenate([td[dz, a, b].astype(F32)] * 2, axis=1) for b in range(3)]
            for a in range(3)
        ]
        for kx in range(4):
            for xp in range(2):
                b = kx - xp
                for slot in range(4):
                    made = none
                    if 0 <= b < 3:
                        low = tiled[slot][b] if slot < 3 else none
                        high = tiled[slot - 1][b] if slot > 0 else none
                        made = jnp.where(lane < 64, low, high)
                    start = 128 * (4 * dz + kx) + 32 * slot
                    wd[start : start + 32, 128 * xp : 128 * xp + 128] = made.astype(BF)

    lane = floor_lane((64, 128), 1)
    heads = jnp.concatenate([small[0:3, :], jnp.zeros((5, 64), F32)], axis=0).T
    for xp in range(2):
        for yp in range(2):
            highs = jnp.zeros((64, 128), F32)
            lows = jnp.zeros((64, 128), F32)
            for k in range(3):
                c = 3 * yp + k
                at = 64 * (c % 2) + 8 * (c // 2) + xp
                column = heads[:, k : k + 1]
                high = column.astype(BF).astype(F32)
                highs = jnp.where(lane == at, high, highs)
                lows = jnp.where(lane == at + 32, column - high, lows)
            for m in range(4):
                start = 512 * m + 64 * (2 * xp + yp)
                both = highs + lows
                wh[start : start + 64, :] = (pltpu.roll(both, 2 * m, 1) if m else both).astype(BF)
                wh[start + 256 : start + 320, :] = (
                    pltpu.roll(highs, 2 * m, 1) if m else highs
                ).astype(BF)


def prepare_deep(small, td):
    shape = jax.ShapeDtypeStruct
    return pl.pallas_call(
        prepare_deep_kernel,
        out_shape=(shape((1536, 256), BF), shape((1, 256), F32), shape((2048, 128), BF)),
        in_specs=[pl.BlockSpec(memory_space=VMEM)] * 2,
        out_specs=[pl.BlockSpec(memory_space=VMEM)] * 3,
        compiler_params=pltpu.CompilerParams(vmem_limit_bytes=8 * 1024 * 1024),
        cost_estimate=pl.CostEstimate(flops=1000000, bytes_accessed=4000000, transcendentals=0),
        name="prepare_deep",
    )(small, td)


def prepare(small, w_first, w_second, ts):
    shape = jax.ShapeDtypeStruct
    return pl.pallas_call(
        prepare_kernel,
        out_shape=(
            shape((128, 2688), BF),
            shape((32, 384), F32),
            shape((768, 256), BF),
            shape((1, 256), F32),
            shape((256, 128), BF),
            shape((1, 128), F32),
        ),
        in_specs=[pl.BlockSpec(memory_space=VMEM)] * 4,
        out_specs=[pl.BlockSpec(memory_space=VMEM)] * 6,
        compiler_params=pltpu.CompilerParams(vmem_limit_bytes=16 * 1024 * 1024),
        cost_estimate=pl.CostEstimate(flops=1000000, bytes_accessed=4000000, transcendentals=0),
        name="prepare",
    )(
        small,
        jnp.transpose(w_first[:, 0], (1, 2, 0)),
        jnp.transpose(w_second, (2, 3, 0, 1)),
        ts,
    )


def local(
    raw_sections,
    shift_cols,
    shift_rows,
    w_first,
    b_first,
    w_second,
    b_second,
    w_stride,
    b_stride,
    w_depth,
    b_depth,
    w_head,
    b_head,
):
    place = jnp.stack([lax.axis_index("tile"), lax.axis_index("sec")])
    spot = jnp.concatenate([shift_cols, shift_rows, place.astype(jnp.int32)])
    small = jnp.concatenate([w_head, b_depth[None]], axis=0)
    deep = prepare_deep(small, jnp.transpose(w_depth, (2, 3, 4, 1, 0)))
    mine, ts, deep = lax.optimization_barrier(
        (stage(raw_sections), jnp.transpose(w_stride, (2, 3, 1, 0)), deep)
    )
    columns = [
        lax.ppermute(raw_sections, "tile", [(i, i ^ (4 * k)) for i in range(TILES)])
        for k in (1, 2, 3)
    ]
    keep, *sends = pick(spot, mine, *columns)
    sends, firsts, seconds = lax.optimization_barrier((sends, w_first, w_second))
    biases = jnp.concatenate([b_first, b_second, b_stride])[None]
    weights = prepare(biases, firsts, seconds, ts)
    pieces = [
        lax.ppermute(send, "tile", [(i, i ^ k) for i in range(TILES)])
        for k, send in zip((1, 2, 3), sends)
    ]
    both, to_chip, ahead = align(spot, keep, *pieces, *weights)
    window = lax.ppermute(
        to_chip, "sec", [(i, ((i + 1) ^ 1) - 1) for i in range(1, SECS - 1)]
    )
    middle, to_core = own(spot, both, ahead, *weights)
    core_side = lax.ppermute(to_core, "sec", [(i, i ^ 1) for i in range(SECS)])
    chip_side = beyond(spot, window, *weights)
    return main(spot, chip_side, core_side, middle, *deep, b_head)


def solution(mesh):
    in_specs = (P("sec", None, "tile"), P("sec"), P("sec")) + (P(),) * 10
    out_specs = P(None, "sec", None, "tile")
    return jax.shard_map(local, mesh=mesh, in_specs=in_specs, out_specs=out_specs, check_vma=False)
```

```python
import jax
import jax.numpy as jnp
from jax import lax
from jax.experimental import pallas as pl
from jax.experimental.pallas import tpu as pltpu
from jax.sharding import PartitionSpec as P

BLK = 16
TILES = 16
SECS = 16
HALO = 4
OFF = -1e30
BF = jnp.bfloat16
F32 = jnp.float32
SG = 11
VMEM = pltpu.VMEM
SMEM = pltpu.SMEM


COLS, ROWS, TILE, SEC = 0, 2, 4, 5


def floor_lane(shape, dim):
    return lax.broadcasted_iota(jnp.int32, shape, dim)


def first_tile_of(tile, shift):
    start = 128 * tile - BLK * shift - HALO
    first = lax.shift_right_arithmetic(start, 7)
    return first, start - first * 128


def chosen(sources, index, z):
    value = sources[0][z]
    for k in range(1, len(sources)):
        value = jnp.where(index == k, sources[k][z], value)
    return value


def stage_kernel(given, out):
    out[...] = given[...]


def stage(raw):
    return pl.pallas_call(
        stage_kernel,
        out_shape=jax.ShapeDtypeStruct(raw.shape, raw.dtype),
        in_specs=[pl.BlockSpec(memory_space=VMEM)],
        out_specs=pl.BlockSpec(memory_space=VMEM),
        compiler_params=pltpu.CompilerParams(vmem_limit_bytes=8 * 1024 * 1024),
        cost_estimate=pl.CostEstimate(flops=0, bytes_accessed=4000000, transcendentals=0),
        name="stage",
    )(raw)


def pick_kernel(spot, mine, two, one, three, keep, send_2, send_1, send_3):
    sources = (mine, one, two, three)
    tile = spot[TILE]
    place = tile & 3
    for z in range(2):
        for step, out in enumerate((keep, send_1, send_2, send_3)):
            goal = tile ^ step
            first, _ = first_tile_of(goal, spot[COLS + z])
            wanted = first + ((place - first) & 3)
            index = (lax.shift_right_arithmetic(tile, 2) ^ lax.shift_right_arithmetic(wanted, 2)) & 3
            out[z] = chosen(sources, index, z)


def pick(spot, *sources):
    return pl.pallas_call(
        pick_kernel,
        out_shape=[jax.ShapeDtypeStruct((2, 128, 128), BF)] * 4,
        in_specs=[pl.BlockSpec(memory_space=SMEM)] + [pl.BlockSpec(memory_space=VMEM)] * 4,
        out_specs=[pl.BlockSpec(memory_space=VMEM)] * 4,
        compiler_params=pltpu.CompilerParams(vmem_limit_bytes=8 * 1024 * 1024),
        cost_estimate=pl.CostEstimate(flops=0, bytes_accessed=16000000, transcendentals=0),
        name="pick",
    )(spot, *sources)


def align_kernel(
    spot, keep, two, one, three, w1, bias1, w2, bias2, ws, biass, both, to_chip, ahead,
    lifted, left, right, feats, second,
):
    sources = (keep, one, two, three)
    tile = spot[TILE]
    lifted[0:32, :] = jnp.zeros((32, 256), F32)
    lifted[160:192, :] = jnp.zeros((32, 256), F32)
    lane = floor_lane((128, 128), 1)
    odd = spot[SEC] & 1
    for z in range(2):
        first, offset = first_tile_of(tile, spot[COLS + z])
        turned = []
        for k in range(3):
            inside = ((first + k >= 0) & (first + k < TILES)).astype(F32)
            value = chosen(sources, (tile ^ (first + k)) & 3, z).astype(F32) * inside
            turned.append(pltpu.roll(value, 128 - offset, 1))
        low = jnp.where(lane < 128 - offset, turned[0], turned[1])
        high = jnp.where(lane < 128 - offset, turned[1], turned[2])
        low = jnp.where((tile == 0) & (lane < HALO), 0.0, low)
        high = jnp.where((tile == TILES - 1) & (lane >= HALO), 0.0, high)
        lifted[32:160, 0:128] = low
        lifted[32:160, 128:256] = high
        base = pl.multiple_of(32 - BLK * spot[ROWS + z], BLK)
        window = lifted[pl.ds(base, 128), :].astype(BF)
        both[z] = window

        @pl.when(odd == z)
        def _():
            to_chip[0] = window

    @pl.when(odd == 1)
    def _():
        front(
            tile, (both[0],), w1, bias1, w2, bias2, ws, biass, left, right, feats, second, ahead
        )


def align(spot, *sources):
    return pl.pallas_call(
        align_kernel,
        out_shape=[jax.ShapeDtypeStruct((n, 128, 256), BF) for n in (2, 1)] + [features(1)],
        in_specs=[pl.BlockSpec(memory_space=SMEM)] + [pl.BlockSpec(memory_space=VMEM)] * 10,
        out_specs=[pl.BlockSpec(memory_space=VMEM)] * 3,
        scratch_shapes=[pltpu.VMEM((192, 256), F32)] + scratch(1),
        compiler_params=pltpu.CompilerParams(vmem_limit_bytes=24 * 1024 * 1024),
        cost_estimate=pl.CostEstimate(flops=0, bytes_accessed=4000000, transcendentals=0),
        name="align",
    )(spot, *sources)


def front(tile, windows, w1, bias1, w2, bias2, ws, biass, left, right, feats, second, strided):
    count = len(windows)
    for side in (left, right):
        side[:, 0:2, :] = jnp.zeros((count, 2, 128), F32)
        side[:, 130:136, :] = jnp.zeros((count, 6, 128), F32)
    lane = floor_lane((32, 128), 1)
    patches = []
    for z in range(count):
        value = windows[z].astype(F32)
        left[z, 2:130, :] = value[:, 0:128]
        right[z, 2:130, :] = value[:, 128:256]
        made = [None] * SG
        for j in range(8):
            low = left[z, pl.ds(j, 32, stride=4), :]
            high = right[z, pl.ds(j, 32, stride=4), :]
            ring = jnp.where(lane < 8, high, low)
            mine = lane // 16 == j
            for g in range(SG):
                source = low if g < SG - 1 else ring
                shift = (16 * j - 12 * g) % 128
                turned = pltpu.roll(source, shift, 1) if shift else source
                made[g] = turned if j == 0 else jnp.where(mine, turned, made[g])
        patches += made
    patch = jnp.concatenate(patches, axis=0).astype(BF)
    groups = count * SG
    low_edge = tile == 0
    high_edge = tile == TILES - 1
    lane = floor_lane((32, 384), 1)
    for q in range(7):
        made = jnp.dot(patch, w1[:, 384 * q : 384 * (q + 1)], preferred_element_type=F32)
        made = jnp.maximum(made.reshape(groups, 32, 384) + bias1[...][None], 0.0)
        feats[:, 384 * q : 384 * (q + 1)] = made.reshape(groups * 32, 384).astype(BF)
        outside = {0: low_edge & (lane < 384), 1: low_edge & (lane < 192)}
        outside.update({5: high_edge & (lane >= 192), 6: high_edge & (lane >= 0)})
        if q in outside:
            for z in range(count):
                g = SG * z + (0 if q < 2 else SG - 1)
                kept = jnp.where(outside[q], 0.0, made[g])
                feats[32 * g : 32 * g + 32, 384 * q : 384 * (q + 1)] = kept.astype(BF)

    for p in range(6):
        made = jnp.dot(
            feats[:, 384 * p : 384 * p + 768], w2[...], preferred_element_type=F32
        )
        second[p] = jnp.maximum(made + bias2[...], 0.0).astype(BF)
    lane = floor_lane((1, 32, 128), 2)
    row = floor_lane((1, 32, 128), 1)
    from_above = (lane < 32) & (row > 0)
    from_below = (lane >= 96) & (row < 31)
    kept = (lane >= 32) & (lane < 96)
    for p in range(6):
        made = jnp.dot(second[p], ws[...], preferred_element_type=F32)
        made = jnp.maximum(made + biass[...], 0.0)
        down = pltpu.roll(made, 1, 0).reshape(groups, 32, 128)
        up = pltpu.roll(made, groups * 32 - 1, 0).reshape(groups, 32, 128)
        made = made.reshape(groups, 32, 128)
        made = jnp.where(kept, made, jnp.where(from_above, down, jnp.where(from_below, up, 0.0)))
        for g in range(groups):
            value = made[g]
            if p == 0 and g % SG == 0:
                value = jnp.where(low_edge, 0.0, value)
            if p == 5 and g % SG == SG - 1:
                value = jnp.where(high_edge, 0.0, value)
            strided[g // SG, p % 2, 3 * (g % SG) + p // 2] = value.astype(BF)


def own_kernel(
    spot, both, ahead, w1, bias1, w2, bias2, ws, biass, out, to_core, left, right, feats, second
):
    tile = spot[TILE]
    odd = spot[SEC] & 1

    @pl.when(odd == 0)
    def _():
        windows = (both[0], both[1])
        front(tile, windows, w1, bias1, w2, bias2, ws, biass, left, right, feats, second, out)
        to_core[0] = out[1]

    @pl.when(odd == 1)
    def _():
        front(
            tile, (both[1],), w1, bias1, w2, bias2, ws, biass,
            left.at[0:1], right.at[0:1], feats.at[0 : SG * 32], second.at[:, 0 : SG * 32], out.at[1:2],
        )
        out[0] = ahead[0]
        to_core[0] = ahead[0]


def scratch(count):
    return [
        pltpu.VMEM((count, 136, 128), F32),
        pltpu.VMEM((count, 136, 128), F32),
        pltpu.VMEM((count * SG * 32, 2688), BF),
        pltpu.VMEM((6, count * SG * 32, 256), BF),
    ]


def features(count):
    return jax.ShapeDtypeStruct((count, 2, 33, 32, 128), BF)


def own(spot, both, ahead, *weights):
    return pl.pallas_call(
        own_kernel,
        out_shape=[features(2), features(1)],
        in_specs=[pl.BlockSpec(memory_space=SMEM)] + [pl.BlockSpec(memory_space=VMEM)] * 8,
        out_specs=[pl.BlockSpec(memory_space=VMEM)] * 2,
        scratch_shapes=scratch(2),
        compiler_params=pltpu.CompilerParams(vmem_limit_bytes=24 * 1024 * 1024),
        cost_estimate=pl.CostEstimate(flops=40000000000, bytes_accessed=4000000, transcendentals=0),
        name="own",
    )(spot, both, ahead, *weights)


def beyond_kernel(
    spot, th, bd, td, window, w1, bias1, w2, bias2, ws, biass, out, wd, biasd, wh,
    left, right, feats, second,
):
    prepare_deep(th, bd, td, wd, biasd, wh)
    sec = spot[SEC]
    front(
        spot[TILE], (window[0],), w1, bias1, w2, bias2, ws, biass, left, right, feats, second, out
    )

    @pl.when((sec == 0) | (sec == SECS - 1))
    def _():
        out[0] = jnp.zeros((2, 33, 32, 128), BF)


def beyond(spot, th, bd, td, window, *weights):
    shape = jax.ShapeDtypeStruct
    return pl.pallas_call(
        beyond_kernel,
        out_shape=[features(1), shape((1536, 256), BF), shape((1, 256), F32), shape((2048, 128), BF)],
        in_specs=[pl.BlockSpec(memory_space=SMEM)] + [pl.BlockSpec(memory_space=VMEM)] * 10,
        out_specs=[pl.BlockSpec(memory_space=VMEM)] * 4,
        scratch_shapes=scratch(1),
        compiler_params=pltpu.CompilerParams(vmem_limit_bytes=24 * 1024 * 1024),
        cost_estimate=pl.CostEstimate(flops=20000000000, bytes_accessed=4000000, transcendentals=0),
        name="beyond",
    )(spot, th, bd, td, window, *weights)


def main_kernel(spot, chip_side, core_side, middle, wd, biasd, wh, bh, out, outer, deeps):
    odd = spot[SEC] & 1
    outer[odd] = chip_side[0]
    outer[1 - odd] = core_side[0]
    for z in range(2):
        for part in range(4):
            blocks = []
            for dz in range(3):
                source = (outer.at[0], middle.at[0], middle.at[1], outer.at[1])[z + dz]
                for kx in range(4):
                    first = kx // 2 + 8 * part
                    blocks.append(source[kx % 2, first : first + 8].reshape(256, 128))
            patch = jnp.concatenate(blocks, axis=1)
            deep = jnp.dot(patch, wd[...], preferred_element_type=F32)
            deep = jnp.maximum(deep + biasd[...], 0.0)
            high = deep.astype(BF)
            low = (deep - high.astype(F32)).astype(BF)
            for m in range(8):
                here = slice(32 * m, 32 * m + 32)
                rows = pl.ds(32 * (8 * z + 2 * part + m // 4), 32)
                at = 512 * (m % 4)
                deeps[rows, at : at + 256] = high[here]
                deeps[rows, at + 256 : at + 512] = low[here]
    block = lax.shift_right_logical(floor_lane((1, 8, 128), 2) & 63, 3)
    for z in range(2):
        logits = jnp.dot(deeps[256 * z : 256 * z + 256], wh[...], preferred_element_type=F32)
        logits = logits + pltpu.roll(logits, 96, 1)
        spots = [jnp.zeros((4, 8, 128), F32)] * 3
        for part in range(8):
            slab = logits[32 * part : 32 * part + 32]
            for i in range(3):
                shift = 8 * (part - i) % 128
                turned = pltpu.roll(slab, shift, 1) if shift else slab
                spots[i] = jnp.where(block == part, turned.reshape(4, 8, 128), spots[i])
        for i in range(3):
            value = spots[i].reshape(32, 128)
            for half in range(2):
                yp, k = divmod(2 * i + half, 3)
                if half == 1:
                    value = pltpu.roll(value, 64, 1)
                out[k, z, pl.ds(yp, 32, stride=2), :] = jax.nn.sigmoid(value[:, 0:64] + bh[k])


def main(spot, chip_side, core_side, middle, *weights):
    return pl.pallas_call(
        main_kernel,
        out_shape=jax.ShapeDtypeStruct((3, 2, 64, 64), F32),
        in_specs=[pl.BlockSpec(memory_space=SMEM)]
        + [pl.BlockSpec(memory_space=VMEM)] * 6
        + [pl.BlockSpec(memory_space=SMEM)],
        out_specs=pl.BlockSpec(memory_space=VMEM),
        scratch_shapes=[pltpu.VMEM((2, 2, 33, 32, 128), BF), pltpu.VMEM((512, 2048), BF)],
        compiler_params=pltpu.CompilerParams(vmem_limit_bytes=24 * 1024 * 1024),
        name="convs",
    )(spot, chip_side, core_side, middle, *weights)


def prepare_kernel(*refs):
    small, t1, t2, ts = refs[:4]
    w1, bias1, w2, bias2, ws, biass = refs[4:]
    b1, b2, bs = (small[:, 32 * i : 32 * i + 32] for i in range(3))
    row = floor_lane((128, 384), 0)
    group = floor_lane((128, 384), 1) // 32
    dy = row // 16 - group % 6
    dx = row % 16 - group // 6
    base = jnp.zeros((128, 384), F32)
    for a in range(3):
        for b in range(3):
            spread = jnp.concatenate([t1[a, b : b + 1, :].astype(F32)] * 12, axis=1)
            base = jnp.where((dy == a) & (dx == b), spread, base)
    for q in range(7):
        turned = pltpu.roll(base, 2 * q, 0) if q else base
        w1[:, 384 * q : 384 * (q + 1)] = turned.astype(BF)
    lone = jnp.concatenate([b1] * 12, axis=1)
    row = floor_lane((32, 384), 0)
    group = floor_lane((32, 384), 1) // 32 % 6
    outside = ((row == 0) & (group == 0)) | ((row == 31) & (group == 5))
    bias1[...] = jnp.where(outside, OFF, lone)
    bias2[...] = jnp.concatenate([b2] * 8, axis=1)
    biass[...] = jnp.concatenate([bs] * 4, axis=1)

    lane = floor_lane((32, 128), 1)
    none = jnp.zeros((32, 128), F32)
    tiled = [
        [jnp.concatenate([t2[a, b].astype(F32).T] * 4, axis=1) for b in range(3)] for a in range(3)
    ]
    for kx in range(4):
        for xp in range(2):
            b = kx - xp
            for j in range(6):
                made = none
                if 0 <= b < 3:
                    for a in range(3):
                        if 0 <= j - a < 4:
                            made = jnp.where(lane // 32 == j - a, tiled[a][b], made)
                start = 32 * (6 * kx + j)
                w2[start : start + 32, 128 * xp : 128 * xp + 128] = made.astype(BF)

    tiled = [
        [jnp.concatenate([ts[a, b].astype(F32)] * 4, axis=1) for b in range(2)] for a in range(2)
    ]
    for xp in range(2):
        for yp in range(4):
            mine = (lane // 32) % 2 == (1 if yp < 2 else 0)
            start = 32 * (4 * xp + yp)
            ws[start : start + 32, :] = jnp.where(mine, tiled[yp % 2][xp], 0.0).astype(BF)


def prepare_deep(th, bd, td, wd, biasd, wh):
    lane = floor_lane((32, 128), 1)
    none = jnp.zeros((32, 128), F32)
    biasd[...] = jnp.concatenate([bd[...]] * 4, axis=1)
    for dz in range(3):
        tiled = [
            [jnp.concatenate([td[dz, a, b].astype(F32)] * 2, axis=1) for b in range(3)]
            for a in range(3)
        ]
        for kx in range(4):
            for xp in range(2):
                b = kx - xp
                for slot in range(4):
                    made = none
                    if 0 <= b < 3:
                        low = tiled[slot][b] if slot < 3 else none
                        high = tiled[slot - 1][b] if slot > 0 else none
                        made = jnp.where(lane < 64, low, high)
                    start = 128 * (4 * dz + kx) + 32 * slot
                    wd[start : start + 32, 128 * xp : 128 * xp + 128] = made.astype(BF)

    lane = floor_lane((64, 128), 1)
    heads = jnp.concatenate([th[...], jnp.zeros((5, 64), F32)], axis=0).T
    for xp in range(2):
        for yp in range(2):
            highs = jnp.zeros((64, 128), F32)
            lows = jnp.zeros((64, 128), F32)
            for k in range(3):
                c = 3 * yp + k
                at = 64 * (c % 2) + 8 * (c // 2) + xp
                column = heads[:, k : k + 1]
                high = column.astype(BF).astype(F32)
                highs = jnp.where(lane == at, high, highs)
                lows = jnp.where(lane == at + 32, column - high, lows)
            for m in range(4):
                start = 512 * m + 64 * (2 * xp + yp)
                both = highs + lows
                wh[start : start + 64, :] = (pltpu.roll(both, 2 * m, 1) if m else both).astype(BF)
                wh[start + 256 : start + 320, :] = (
                    pltpu.roll(highs, 2 * m, 1) if m else highs
                ).astype(BF)


def prepare(small, w_first, w_second, ts):
    shape = jax.ShapeDtypeStruct
    return pl.pallas_call(
        prepare_kernel,
        out_shape=(
            shape((128, 2688), BF),
            shape((32, 384), F32),
            shape((768, 256), BF),
            shape((1, 256), F32),
            shape((256, 128), BF),
            shape((1, 128), F32),
        ),
        in_specs=[pl.BlockSpec(memory_space=VMEM)] * 4,
        out_specs=[pl.BlockSpec(memory_space=VMEM)] * 6,
        compiler_params=pltpu.CompilerParams(vmem_limit_bytes=16 * 1024 * 1024),
        cost_estimate=pl.CostEstimate(flops=1000000, bytes_accessed=4000000, transcendentals=0),
        name="prepare",
    )(
        small,
        jnp.transpose(w_first[:, 0], (1, 2, 0)),
        jnp.transpose(w_second, (2, 3, 0, 1)),
        ts,
    )


def local(
    raw_sections,
    shift_cols,
    shift_rows,
    w_first,
    b_first,
    w_second,
    b_second,
    w_stride,
    b_stride,
    w_depth,
    b_depth,
    w_head,
    b_head,
):
    place = jnp.stack([lax.axis_index("tile"), lax.axis_index("sec")])
    spot = jnp.concatenate([shift_cols, shift_rows, place.astype(jnp.int32)])
    mine, ts = lax.optimization_barrier((stage(raw_sections), jnp.transpose(w_stride, (2, 3, 1, 0))))
    far, near, around = (
        lax.ppermute(raw_sections, "tile", [(i, i ^ (4 * k)) for i in range(TILES)])
        for k in (2, 1, 3)
    )
    columns = (far, near, around)
    keep, *sends = pick(spot, mine, *columns)
    sends, firsts, seconds = lax.optimization_barrier((sends, w_first, w_second))
    biases = jnp.concatenate([b_first, b_second, b_stride])[None]
    weights = prepare(biases, firsts, seconds, ts)
    pieces = [
        lax.ppermute(send, "tile", [(i, i ^ k) for i in range(TILES)])
        for k, send in zip((2, 1, 3), sends)
    ]
    both, to_chip, ahead = align(spot, keep, *pieces, *weights)
    window = lax.ppermute(
        to_chip, "sec", [(i, ((i + 1) ^ 1) - 1) for i in range(1, SECS - 1)]
    )
    middle, to_core = own(spot, both, ahead, *weights)
    core_side = lax.ppermute(to_core, "sec", [(i, i ^ 1) for i in range(SECS)])
    td = jnp.transpose(w_depth, (2, 3, 4, 1, 0))
    chip_side, *deep = beyond(spot, w_head, b_depth[None], td, window, *weights)
    return main(spot, chip_side, core_side, middle, *deep, b_head)


def solution(mesh):
    in_specs = (P("sec", None, "tile"), P("sec"), P("sec")) + (P(),) * 10
    out_specs = P(None, "sec", None, "tile")
    return jax.shard_map(local, mesh=mesh, in_specs=in_specs, out_specs=out_specs, check_vma=False)
```

```python
import jax
import jax.numpy as jnp
from jax import lax
from jax.experimental import pallas as pl
from jax.experimental.pallas import tpu as pltpu
from jax.sharding import PartitionSpec as P

BLK = 16
TILES = 16
SECS = 16
HALO = 4
OFF = -1e30
BF = jnp.bfloat16
F32 = jnp.float32
SG = 11
VMEM = pltpu.VMEM
SMEM = pltpu.SMEM


COLS, ROWS, TILE, SEC = 0, 2, 4, 5


def floor_lane(shape, dim):
    return lax.broadcasted_iota(jnp.int32, shape, dim)


def first_tile_of(tile, shift):
    start = 128 * tile - BLK * shift - HALO
    first = lax.shift_right_arithmetic(start, 7)
    return first, start - first * 128


def chosen(sources, index, z):
    value = sources[0][z]
    for k in range(1, len(sources)):
        value = jnp.where(index == k, sources[k][z], value)
    return value


def stage_kernel(given, out):
    out[...] = given[...]


def stage(raw):
    return pl.pallas_call(
        stage_kernel,
        out_shape=jax.ShapeDtypeStruct(raw.shape, raw.dtype),
        in_specs=[pl.BlockSpec(memory_space=VMEM)],
        out_specs=pl.BlockSpec(memory_space=VMEM),
        compiler_params=pltpu.CompilerParams(vmem_limit_bytes=8 * 1024 * 1024),
        cost_estimate=pl.CostEstimate(flops=0, bytes_accessed=4000000, transcendentals=0),
        name="stage",
    )(raw)


def pick_kernel(spot, mine, two, one, three, keep, send_2, send_1, send_3):
    sources = (mine, one, two, three)
    tile = spot[TILE]
    place = tile & 3
    for z in range(2):
        for step, out in enumerate((keep, send_1, send_2, send_3)):
            goal = tile ^ step
            first, _ = first_tile_of(goal, spot[COLS + z])
            wanted = first + ((place - first) & 3)
            index = (lax.shift_right_arithmetic(tile, 2) ^ lax.shift_right_arithmetic(wanted, 2)) & 3
            out[z] = chosen(sources, index, z)


def pick(spot, *sources):
    return pl.pallas_call(
        pick_kernel,
        out_shape=[jax.ShapeDtypeStruct((2, 128, 128), BF)] * 4,
        in_specs=[pl.BlockSpec(memory_space=SMEM)] + [pl.BlockSpec(memory_space=VMEM)] * 4,
        out_specs=[pl.BlockSpec(memory_space=VMEM)] * 4,
        compiler_params=pltpu.CompilerParams(vmem_limit_bytes=8 * 1024 * 1024),
        cost_estimate=pl.CostEstimate(flops=0, bytes_accessed=16000000, transcendentals=0),
        name="pick",
    )(spot, *sources)


def align_kernel(
    spot, keep, two, one, three, w1, bias1, w2, bias2, ws, biass, both, to_chip, ahead,
    lifted, left, right, feats, second,
):
    sources = (keep, one, two, three)
    tile = spot[TILE]
    lifted[0:32, :] = jnp.zeros((32, 256), F32)
    lifted[160:192, :] = jnp.zeros((32, 256), F32)
    lane = floor_lane((128, 128), 1)
    odd = spot[SEC] & 1
    for z in range(2):
        first, offset = first_tile_of(tile, spot[COLS + z])
        turned = []
        for k in range(3):
            inside = ((first + k >= 0) & (first + k < TILES)).astype(F32)
            value = chosen(sources, (tile ^ (first + k)) & 3, z).astype(F32) * inside
            turned.append(pltpu.roll(value, 128 - offset, 1))
        low = jnp.where(lane < 128 - offset, turned[0], turned[1])
        high = jnp.where(lane < 128 - offset, turned[1], turned[2])
        low = jnp.where((tile == 0) & (lane < HALO), 0.0, low)
        high = jnp.where((tile == TILES - 1) & (lane >= HALO), 0.0, high)
        lifted[32:160, 0:128] = low
        lifted[32:160, 128:256] = high
        base = pl.multiple_of(32 - BLK * spot[ROWS + z], BLK)
        window = lifted[pl.ds(base, 128), :].astype(BF)
        both[z] = window

        @pl.when(odd == z)
        def _():
            to_chip[0] = window

    @pl.when(odd == 1)
    def _():
        front(
            tile, (both[0],), w1, bias1, w2, bias2, ws, biass, left, right, feats, second, (ahead,)
        )


def align(spot, *sources):
    return pl.pallas_call(
        align_kernel,
        out_shape=[jax.ShapeDtypeStruct((n, 128, 256), BF) for n in (2, 1)] + [features(1)],
        in_specs=[pl.BlockSpec(memory_space=SMEM)] + [pl.BlockSpec(memory_space=VMEM)] * 10,
        out_specs=[pl.BlockSpec(memory_space=VMEM)] * 3,
        scratch_shapes=[pltpu.VMEM((192, 256), F32)] + scratch(1),
        compiler_params=pltpu.CompilerParams(vmem_limit_bytes=24 * 1024 * 1024),
        cost_estimate=pl.CostEstimate(flops=0, bytes_accessed=4000000, transcendentals=0),
        name="align",
    )(spot, *sources)


def front(tile, windows, w1, bias1, w2, bias2, ws, biass, left, right, feats, second, strided):
    count = len(windows)
    for side in (left, right):
        side[:, 0:2, :] = jnp.zeros((count, 2, 128), F32)
        side[:, 130:136, :] = jnp.zeros((count, 6, 128), F32)
    lane = floor_lane((32, 128), 1)
    patches = []
    for z in range(count):
        value = windows[z].astype(F32)
        left[z, 2:130, :] = value[:, 0:128]
        right[z, 2:130, :] = value[:, 128:256]
        made = [None] * SG
        for j in range(8):
            low = left[z, pl.ds(j, 32, stride=4), :]
            high = right[z, pl.ds(j, 32, stride=4), :]
            ring = jnp.where(lane < 8, high, low)
            mine = lane // 16 == j
            for g in range(SG):
                source = low if g < SG - 1 else ring
                shift = (16 * j - 12 * g) % 128
                turned = pltpu.roll(source, shift, 1) if shift else source
                made[g] = turned if j == 0 else jnp.where(mine, turned, made[g])
        patches += made
    patch = jnp.concatenate(patches, axis=0).astype(BF)
    groups = count * SG
    low_edge = tile == 0
    high_edge = tile == TILES - 1
    lane = floor_lane((32, 384), 1)
    for q in range(7):
        made = jnp.dot(patch, w1[:, 384 * q : 384 * (q + 1)], preferred_element_type=F32)
        made = jnp.maximum(made.reshape(groups, 32, 384) + bias1[...][None], 0.0)
        feats[:, 384 * q : 384 * (q + 1)] = made.reshape(groups * 32, 384).astype(BF)
        outside = {0: low_edge & (lane < 384), 1: low_edge & (lane < 192)}
        outside.update({5: high_edge & (lane >= 192), 6: high_edge & (lane >= 0)})
        if q in outside:
            for z in range(count):
                g = SG * z + (0 if q < 2 else SG - 1)
                kept = jnp.where(outside[q], 0.0, made[g])
                feats[32 * g : 32 * g + 32, 384 * q : 384 * (q + 1)] = kept.astype(BF)

    for p in range(6):
        made = jnp.dot(
            feats[:, 384 * p : 384 * p + 768], w2[...], preferred_element_type=F32
        )
        second[p] = jnp.maximum(made + bias2[...], 0.0).astype(BF)
    lane = floor_lane((1, 32, 128), 2)
    row = floor_lane((1, 32, 128), 1)
    from_above = (lane < 32) & (row > 0)
    from_below = (lane >= 96) & (row < 31)
    kept = (lane >= 32) & (lane < 96)
    for p in range(6):
        made = jnp.dot(second[p], ws[...], preferred_element_type=F32)
        made = jnp.maximum(made + biass[...], 0.0)
        down = pltpu.roll(made, 1, 0).reshape(groups, 32, 128)
        up = pltpu.roll(made, groups * 32 - 1, 0).reshape(groups, 32, 128)
        made = made.reshape(groups, 32, 128)
        made = jnp.where(kept, made, jnp.where(from_above, down, jnp.where(from_below, up, 0.0)))
        for g in range(groups):
            value = made[g]
            if p == 0 and g % SG == 0:
                value = jnp.where(low_edge, 0.0, value)
            if p == 5 and g % SG == SG - 1:
                value = jnp.where(high_edge, 0.0, value)
            strided[g // SG][0, p % 2, 3 * (g % SG) + p // 2] = value.astype(BF)


def own_kernel(
    spot, both, ahead, w1, bias1, w2, bias2, ws, biass, near, inner, left, right, feats, second
):
    tile = spot[TILE]
    odd = spot[SEC] & 1

    @pl.when(odd == 0)
    def _():
        windows = (both[0], both[1])
        front(
            tile, windows, w1, bias1, w2, bias2, ws, biass, left, right, feats, second, (near, inner)
        )

    @pl.when(odd == 1)
    def _():
        front(
            tile, (both[1],), w1, bias1, w2, bias2, ws, biass,
            left.at[0:1], right.at[0:1], feats.at[0 : SG * 32], second.at[:, 0 : SG * 32], (near,),
        )
        inner[0] = ahead[0]


def scratch(count):
    return [
        pltpu.VMEM((count, 136, 128), F32),
        pltpu.VMEM((count, 136, 128), F32),
        pltpu.VMEM((count * SG * 32, 2688), BF),
        pltpu.VMEM((6, count * SG * 32, 256), BF),
    ]


def features(count):
    return jax.ShapeDtypeStruct((count, 2, 33, 32, 128), BF)


def own(spot, both, ahead, *weights):
    return pl.pallas_call(
        own_kernel,
        out_shape=[features(1), features(1)],
        in_specs=[pl.BlockSpec(memory_space=SMEM)] + [pl.BlockSpec(memory_space=VMEM)] * 8,
        out_specs=[pl.BlockSpec(memory_space=VMEM)] * 2,
        scratch_shapes=scratch(2),
        compiler_params=pltpu.CompilerParams(vmem_limit_bytes=24 * 1024 * 1024),
        cost_estimate=pl.CostEstimate(flops=40000000000, bytes_accessed=4000000, transcendentals=0),
        name="own",
    )(spot, both, ahead, *weights)


def beyond_kernel(
    spot, window, w1, bias1, w2, bias2, ws, biass, out, left, right, feats, second
):
    sec = spot[SEC]
    front(
        spot[TILE], (window[0],), w1, bias1, w2, bias2, ws, biass, left, right, feats, second, (out,)
    )

    @pl.when((sec == 0) | (sec == SECS - 1))
    def _():
        out[0] = jnp.zeros((2, 33, 32, 128), BF)


def beyond(spot, window, *weights):
    return pl.pallas_call(
        beyond_kernel,
        out_shape=features(1),
        in_specs=[pl.BlockSpec(memory_space=SMEM)] + [pl.BlockSpec(memory_space=VMEM)] * 7,
        out_specs=pl.BlockSpec(memory_space=VMEM),
        scratch_shapes=scratch(1),
        compiler_params=pltpu.CompilerParams(vmem_limit_bytes=24 * 1024 * 1024),
        cost_estimate=pl.CostEstimate(flops=20000000000, bytes_accessed=4000000, transcendentals=0),
        name="beyond",
    )(spot, window, *weights)


def main_kernel(spot, beyond, near, inner, mate, wd, biasd, wh, bh, out, deeps):
    odd = spot[SEC] & 1
    order = (beyond, near, inner, mate)
    for z in range(2):
        for part in range(4):
            deep = biasd[...]
            for dz in range(3):
                source = order[z + dz].at[0]
                blocks = []
                for kx in range(4):
                    first = kx // 2 + 8 * part
                    blocks.append(source[kx % 2, first : first + 8].reshape(256, 128))
                patch = jnp.concatenate(blocks, axis=1)
                layer = pl.multiple_of(512 * jnp.where(odd == 1, 2 - dz, dz), 512)
                deep += jnp.dot(patch, wd[pl.ds(layer, 512), :], preferred_element_type=F32)
            deep = jnp.maximum(deep, 0.0)
            high = deep.astype(BF)
            low = (deep - high.astype(F32)).astype(BF)
            for m in range(8):
                here = slice(32 * m, 32 * m + 32)
                rows = pl.ds(32 * (8 * z + 2 * part + m // 4), 32)
                at = 512 * (m % 4)
                deeps[rows, at : at + 256] = high[here]
                deeps[rows, at + 256 : at + 512] = low[here]
    block = lax.shift_right_logical(floor_lane((1, 8, 128), 2) & 63, 3)
    for z in range(2):
        logits = jnp.dot(deeps[256 * z : 256 * z + 256], wh[...], preferred_element_type=F32)
        logits = logits + pltpu.roll(logits, 96, 1)
        spots = [jnp.zeros((4, 8, 128), F32)] * 3
        for part in range(8):
            slab = logits[32 * part : 32 * part + 32]
            for i in range(3):
                shift = 8 * (part - i) % 128
                turned = pltpu.roll(slab, shift, 1) if shift else slab
                spots[i] = jnp.where(block == part, turned.reshape(4, 8, 128), spots[i])
        goal = jnp.where(odd == 1, 1 - z, z)
        for i in range(3):
            value = spots[i].reshape(32, 128)
            for half in range(2):
                yp, k = divmod(2 * i + half, 3)
                if half == 1:
                    value = pltpu.roll(value, 64, 1)
                out[k, goal, pl.ds(yp, 32, stride=2), :] = jax.nn.sigmoid(value[:, 0:64] + bh[0:1, 64 + k : 65 + k])


def main(spot, beyond, near, inner, mate, *weights):
    return pl.pallas_call(
        main_kernel,
        out_shape=jax.ShapeDtypeStruct((3, 2, 64, 64), F32),
        in_specs=[pl.BlockSpec(memory_space=SMEM)]
        + [pl.BlockSpec(memory_space=VMEM)] * 8,
        out_specs=pl.BlockSpec(memory_space=VMEM),
        scratch_shapes=[pltpu.VMEM((512, 2048), BF)],
        compiler_params=pltpu.CompilerParams(vmem_limit_bytes=24 * 1024 * 1024),
        name="convs",
    )(spot, beyond, near, inner, mate, *weights)


def prepare_kernel(*refs):
    small, t1, t2, ts, th, td = refs[:6]
    w1, bias1, w2, bias2, ws, biass, tail, wd, biasd, wh = refs[6:]
    tail[:, 0:67] = small[:, 96:163]
    prepare_deep(th, tail, td, wd, biasd, wh)
    b1, b2, bs = (small[:, 32 * i : 32 * i + 32] for i in range(3))
    row = floor_lane((128, 384), 0)
    group = floor_lane((128, 384), 1) // 32
    dy = row // 16 - group % 6
    dx = row % 16 - group // 6
    base = jnp.zeros((128, 384), F32)
    for a in range(3):
        for b in range(3):
            spread = jnp.concatenate([t1[a, b : b + 1, :].astype(F32)] * 12, axis=1)
            base = jnp.where((dy == a) & (dx == b), spread, base)
    for q in range(7):
        turned = pltpu.roll(base, 2 * q, 0) if q else base
        w1[:, 384 * q : 384 * (q + 1)] = turned.astype(BF)
    lone = jnp.concatenate([b1] * 12, axis=1)
    row = floor_lane((32, 384), 0)
    group = floor_lane((32, 384), 1) // 32 % 6
    outside = ((row == 0) & (group == 0)) | ((row == 31) & (group == 5))
    bias1[...] = jnp.where(outside, OFF, lone)
    bias2[...] = jnp.concatenate([b2] * 8, axis=1)
    biass[...] = jnp.concatenate([bs] * 4, axis=1)

    lane = floor_lane((32, 128), 1)
    none = jnp.zeros((32, 128), F32)
    tiled = [
        [jnp.concatenate([t2[a, b].astype(F32).T] * 4, axis=1) for b in range(3)] for a in range(3)
    ]
    for kx in range(4):
        for xp in range(2):
            b = kx - xp
            for j in range(6):
                made = none
                if 0 <= b < 3:
                    for a in range(3):
                        if 0 <= j - a < 4:
                            made = jnp.where(lane // 32 == j - a, tiled[a][b], made)
                start = 32 * (6 * kx + j)
                w2[start : start + 32, 128 * xp : 128 * xp + 128] = made.astype(BF)

    tiled = [
        [jnp.concatenate([ts[a, b].astype(F32)] * 4, axis=1) for b in range(2)] for a in range(2)
    ]
    for xp in range(2):
        for yp in range(4):
            mine = (lane // 32) % 2 == (1 if yp < 2 else 0)
            start = 32 * (4 * xp + yp)
            ws[start : start + 32, :] = jnp.where(mine, tiled[yp % 2][xp], 0.0).astype(BF)


def prepare_deep(th, bd, td, wd, biasd, wh):
    lane = floor_lane((32, 128), 1)
    none = jnp.zeros((32, 128), F32)
    biasd[...] = jnp.concatenate([bd[:, 0:64]] * 4, axis=1)
    for dz in range(3):
        tiled = [
            [jnp.concatenate([td[dz, a, b].astype(F32)] * 2, axis=1) for b in range(3)]
            for a in range(3)
        ]
        for kx in range(4):
            for xp in range(2):
                b = kx - xp
                for slot in range(4):
                    made = none
                    if 0 <= b < 3:
                        low = tiled[slot][b] if slot < 3 else none
                        high = tiled[slot - 1][b] if slot > 0 else none
                        made = jnp.where(lane < 64, low, high)
                    start = 128 * (4 * dz + kx) + 32 * slot
                    wd[start : start + 32, 128 * xp : 128 * xp + 128] = made.astype(BF)

    lane = floor_lane((64, 128), 1)
    heads = jnp.concatenate([th[...], jnp.zeros((5, 64), F32)], axis=0).T
    for xp in range(2):
        for yp in range(2):
            highs = jnp.zeros((64, 128), F32)
            lows = jnp.zeros((64, 128), F32)
            for k in range(3):
                c = 3 * yp + k
                at = 64 * (c % 2) + 8 * (c // 2) + xp
                column = heads[:, k : k + 1]
                high = column.astype(BF).astype(F32)
                highs = jnp.where(lane == at, high, highs)
                lows = jnp.where(lane == at + 32, column - high, lows)
            for m in range(4):
                start = 512 * m + 64 * (2 * xp + yp)
                both = highs + lows
                wh[start : start + 64, :] = (pltpu.roll(both, 2 * m, 1) if m else both).astype(BF)
                wh[start + 256 : start + 320, :] = (
                    pltpu.roll(highs, 2 * m, 1) if m else highs
                ).astype(BF)


def prepare(small, w_first, w_second, ts, w_head, w_depth):
    shape = jax.ShapeDtypeStruct
    return pl.pallas_call(
        prepare_kernel,
        out_shape=(
            shape((128, 2688), BF),
            shape((32, 384), F32),
            shape((768, 256), BF),
            shape((1, 256), F32),
            shape((256, 128), BF),
            shape((1, 128), F32),
            shape((1, 128), F32),
            shape((1536, 256), BF),
            shape((1, 256), F32),
            shape((2048, 128), BF),
        ),
        in_specs=[pl.BlockSpec(memory_space=VMEM)] * 6,
        out_specs=[pl.BlockSpec(memory_space=VMEM)] * 10,
        compiler_params=pltpu.CompilerParams(vmem_limit_bytes=16 * 1024 * 1024),
        cost_estimate=pl.CostEstimate(flops=1000000, bytes_accessed=4000000, transcendentals=0),
        name="prepare",
    )(
        small,
        jnp.transpose(w_first[:, 0], (1, 2, 0)),
        jnp.transpose(w_second, (2, 3, 0, 1)),
        ts,
        w_head,
        jnp.transpose(w_depth, (2, 3, 4, 1, 0)),
    )


def local(
    raw_sections,
    shift_cols,
    shift_rows,
    w_first,
    b_first,
    w_second,
    b_second,
    w_stride,
    b_stride,
    w_depth,
    b_depth,
    w_head,
    b_head,
):
    place = jnp.stack([lax.axis_index("tile"), lax.axis_index("sec")])
    spot = jnp.concatenate([shift_cols, shift_rows, place.astype(jnp.int32)])
    mine, ts = lax.optimization_barrier((stage(raw_sections), jnp.transpose(w_stride, (2, 3, 1, 0))))
    far, near, around = (
        lax.ppermute(raw_sections, "tile", [(i, i ^ (4 * k)) for i in range(TILES)])
        for k in (2, 1, 3)
    )
    columns = (far, near, around)
    keep, *sends = pick(spot, mine, *columns)
    sends, firsts, seconds, heads, depths = lax.optimization_barrier(
        (sends, w_first, w_second, w_head, w_depth)
    )
    biases = jnp.concatenate([b_first, b_second, b_stride, b_depth, b_head])[None]
    *weights, tail, wd, biasd, wh = prepare(biases, firsts, seconds, ts, heads, depths)
    pieces = [
        lax.ppermute(send, "tile", [(i, i ^ k) for i in range(TILES)])
        for k, send in zip((2, 1, 3), sends)
    ]
    both, to_chip, ahead = align(spot, keep, *pieces, *weights)
    window = lax.ppermute(
        to_chip, "sec", [(i, ((i + 1) ^ 1) - 1) for i in range(1, SECS - 1)]
    )
    near, inner = own(spot, both, ahead, *weights)
    mate = lax.ppermute(inner, "sec", [(i, i ^ 1) for i in range(SECS)])
    chip_side = beyond(spot, window, *weights)
    return main(spot, chip_side, near, inner, mate, wd, biasd, wh, tail)


def solution(mesh):
    in_specs = (P("sec", None, "tile"), P("sec"), P("sec")) + (P(),) * 10
    out_specs = P(None, "sec", None, "tile")
    return jax.shard_map(local, mesh=mesh, in_specs=in_specs, out_specs=out_specs, check_vma=False)
```
